512 devices in a mesh: section: 8 (over y, core), dp: 32 (over z, x_hi), grp: 2 (over x_lo).
Axes of the slice: x: 4 (x_hi: 2, x_lo: 2; x = x_hi * 2 + x_lo), y: 4, z: 16, core: 2. Of those that a mesh axis runs over, the one named last changes fastest.
Arguments:
- hidden: bfloat16 [14336, 14336], P('dp', ('section', 'grp')), may hold values from -6 to 6
- residual: bfloat16 [14336, 4096], P('dp', ('section', 'grp')), may hold values from -6 to 6
- down_weight: bfloat16 [14336, 4096], P(('section', 'grp'), 'dp'), may hold values from -0.09375 to 0.09375
- norm_gain: float32 [4096], replicated, may hold values from 0.3 to 3
- seq_lengths: int32 [32, 32], P('dp'), may hold values from 1 to 64, 448 in all within a row
- owner_slot: int32 [32, 32], P('dp'), may hold values from 0 to 31, each once within a row
- student_emb: bfloat16 [1024, 1024], P('dp'), may hold values from -6 to 6
- proj_weight: bfloat16 [1024, 4096], P(None, ('section', 'grp')), may hold values from -0.1875 to 0.1875
Outputs:
- grad_proj: float32 [1024, 4096], P(None, ('section', 'grp'))
- grad_student: float32 [1024, 1024], P('dp')
- loss: float32 [], replicated
The draws below stay inside these ranges and needn't reach their ends.
Inputs may be any that keep to these rules, and one draw needn't show every extreme that they name: Each row of owner_slot holds every number of 0 to 31 once. `seq_lengths`: each row sums to 448; some entry of each row equals 64.
All inputs are finite; a program needn't handle non-finite values.
Results may differ from the reference program's by a relative error of at most 0.015.
Values may be sent and summed in bfloat16 or wider, within the bound.
No kernel may reach another device: no remote copies, remote signals or barrier semaphores. Data moves between devices by JAX's collectives and lax.ppermute only.
A program may use at most 64 MiB of HBM per device.

```python
import math
import jax
import jax.numpy as jnp
import numpy as np
from jax import lax

D = 4096
FF = 14336
DS = 1024
LMAX = 64
TOK_DEV = 448
SEQ = 32
TOKENS = 14336
BATCH = 1024
N_SECTION = 8
N_DP = 32
N_GRP = 2


def spiked(values, stream_key, source, target, parts, factor):
    owner, partner = [(jnp.arange(values.shape[position]) // (values.shape[position] // parts)).reshape([-1 if axis == position else 1 for axis in range(values.ndim)]) for position in (source, target)]
    chosen = jax.random.permutation(stream_key, parts)[partner]
    strong = (owner == chosen) | (owner == (partner + parts // 2) % parts)
    return jnp.where(strong, factor * values, values)


def level_of(stream_key, shape, shards, smallest, top_value):
    gain = 1.0
    for axis_at, parts in shards:
        steps = jax.random.uniform(jax.random.fold_in(jax.random.fold_in(stream_key, 6), axis_at), (parts,), jnp.float32, smallest / len(shards), top_value / len(shards))
        gain = gain * jnp.repeat(jnp.exp(steps), shape[axis_at] // parts).reshape((-1,) + (1,) * (len(shape) - 1 - axis_at))
    return gain


def length_profile(amount, total, bound, skew):
    weights = [(1 << 20) // math.isqrt(rank ** skew) + 1 for rank in range(2, amount + 1)]
    surplus, counts = total - bound - (amount - 1), [1] * (amount - 1)
    while surplus > 0:
        free = [i for i in range(amount - 1) if counts[i] < bound]
        whole, remaining = sum([weights[i] for i in free]), surplus
        for i in free:
            extra = min(bound - counts[i], max(1, remaining * weights[i] // whole), surplus)
            counts[i] = counts[i] + extra
            surplus = surplus - extra
    return np.array([bound] + counts)


def ragged(rng, count, total, reach, lean):
    if count == 2:
        one = jax.random.randint(rng, (), max(1, total - reach), min(reach, total - 1) + 1)
        return jnp.stack([one, total - one])
    sizes = jnp.asarray(length_profile(count, total, reach, lean), jnp.int32)
    pairs = (count - 1) // 2
    source_of, sink = sizes[1:1 + 2 * pairs:2], sizes[2:2 + 2 * pairs:2]
    room = jnp.minimum(source_of - 1, reach - sink)
    passed = jax.random.randint(jax.random.fold_in(rng, 1), (pairs,), 0, 1 << 20) % (room + 1)
    sizes = sizes.at[1:1 + 2 * pairs:2].set(source_of - passed).at[2:2 + 2 * pairs:2].set(sink + passed)
    return sizes[jax.random.permutation(jax.random.fold_in(rng, 2), count)]


def noise(stream_key, shape, scale, bound, pieces=(), kind=jnp.bfloat16):
    result = scale * jax.random.normal(stream_key, shape, jnp.float32)
    if pieces:
        result = result * level_of(stream_key, shape, pieces, -0.22, 0.18)
    return jnp.clip(result, -bound, bound).astype(kind)


def heavy_noise(rng, extent, deviation, most, cuts, heavy, held_as=jnp.bfloat16):
    entries = deviation * jax.random.normal(rng, extent, jnp.float32)
    if cuts:
        entries = entries * level_of(rng, extent, cuts, -0.22, 0.18)
    return jnp.clip(spiked(entries, jax.random.fold_in(rng, 3), *heavy), -most, most).astype(held_as)


def setup_inputs(seed: int = 0) -> dict:
    key_of = jax.random.split(jax.random.key(seed), 9)
    hidden = noise(key_of[0], (TOKENS, FF), 1.0, 6.0, ((0, 32), (1, 16)))
    residual = noise(key_of[1], (TOKENS, D), 1.0, 6.0, ((0, 32), (1, 16)))
    down_weight = heavy_noise(key_of[2], (FF, D), FF ** -0.5, 0.09375, ((0, 16), (1, 32)), (0, 1, 32, 2.75))
    norm_gain = jnp.clip(jnp.exp(jax.random.uniform(key_of[3], (D,), jnp.float32, math.log(0.3), math.log(3.0))), 0.3, 3.0)
    seq_lengths = jax.vmap(lambda own: ragged(own, SEQ, TOK_DEV, LMAX, 2))(jax.random.split(key_of[4], N_DP)).reshape((N_DP, SEQ)).astype(jnp.int32)
    owner_slot = jax.vmap(lambda own: jax.random.permutation(own, SEQ))(jax.random.split(key_of[5], N_DP)).reshape((N_DP, SEQ)).astype(jnp.int32)
    student_emb = noise(key_of[6], (BATCH, DS), 1.0, 6.0, ((0, 32),))
    proj_weight = noise(key_of[7], (DS, D), DS ** -0.5, 0.1875, ((1, 16),))
    return {"hidden": hidden, "residual": residual, "down_weight": down_weight, "norm_gain": norm_gain, "seq_lengths": seq_lengths, "owner_slot": owner_slot, "student_emb": student_emb, "proj_weight": proj_weight}


grad_scale = 262144.0

def reference(hidden, residual, down_weight, norm_gain, seq_lengths, owner_slot, student_emb, proj_weight):
    groups = N_SECTION * N_GRP
    share = FF // groups
    weight_parts = down_weight.reshape(groups, share, D)

    def teacher_group(items):
        hid, res, lens, owner = items
        hid_parts = hid.reshape(TOK_DEV, groups, share).transpose(1, 0, 2)

        def add_part(total, pair):
            piece, weight = pair
            term = jnp.dot(piece, weight, preferred_element_type=jnp.float32).astype(jnp.bfloat16)
            term = lax.optimization_barrier(term)
            return (total + term.astype(jnp.float32), None)
        start = jnp.zeros((TOK_DEV, D), jnp.float32)
        summed, _ = lax.scan(add_part, start, (hid_parts, weight_parts))
        y = summed + res.astype(jnp.float32)
        mean_sq = lax.optimization_barrier(jnp.mean(y * y, axis=1))
        normed = (y * lax.rsqrt(mean_sq + 1e-05)[:, None] * norm_gain).astype(jnp.bfloat16)
        places = jnp.arange(TOK_DEV, dtype=jnp.int32)
        starts = jnp.cumsum(lens).astype(jnp.int32) - lens
        member = ((places[None, :] >= starts[:, None]) & (places[None, :] < (starts + lens)[:, None])).astype(jnp.bfloat16)
        sums = jnp.dot(member, normed, preferred_element_type=jnp.float32)
        pooled = (sums / lens[:, None].astype(jnp.float32)).astype(jnp.bfloat16)
        select = (owner[None, :] == jnp.arange(SEQ, dtype=jnp.int32)[:, None]).astype(jnp.bfloat16)
        return jnp.dot(select, pooled, preferred_element_type=jnp.float32).astype(jnp.bfloat16)
    sent = lax.map(teacher_group, (hidden.reshape(N_DP, TOK_DEV, FF), residual.reshape(N_DP, TOK_DEV, D), seq_lengths, owner_slot))
    teacher_rows = sent.reshape(N_DP, N_DP, SEQ // N_DP, D).transpose(1, 0, 2, 3).reshape(BATCH, D)
    u = jnp.dot(student_emb, proj_weight, preferred_element_type=jnp.float32)
    tch = teacher_rows.astype(jnp.float32)
    root = jnp.sqrt(jnp.float32(D))
    rms_u = jnp.sqrt(lax.optimization_barrier(jnp.mean(u * u, axis=1)) + 1e-06)
    rms_t = jnp.sqrt(lax.optimization_barrier(jnp.mean(tch * tch, axis=1)) + 1e-06)
    uhat = u / (root * rms_u[:, None])
    that = tch / (root * rms_t[:, None])
    cosv = lax.optimization_barrier(jnp.sum(uhat * that, axis=1))
    uhat_b = uhat.astype(jnp.bfloat16)
    that_b = that.astype(jnp.bfloat16)
    gram_u = jnp.dot(uhat_b, uhat_b.T, preferred_element_type=jnp.float32)
    gram_t = jnp.dot(that_b, that_b.T, preferred_element_type=jnp.float32)
    diff = gram_u - gram_t
    loss = jnp.mean(1.0 - cosv) + jnp.sum(diff * diff) / BATCH
    diff_b = diff.astype(jnp.bfloat16)
    grad_hat = grad_scale * (-that / BATCH + 4.0 / BATCH * jnp.dot(diff_b, uhat_b, preferred_element_type=jnp.float32))
    inner = lax.optimization_barrier(jnp.sum(grad_hat * uhat, axis=1))
    du = ((grad_hat - uhat * inner[:, None]) / (root * rms_u[:, None])).astype(jnp.bfloat16)
    grad_proj = jnp.dot(student_emb.T, du, preferred_element_type=jnp.float32)
    grad_student = jnp.dot(du, proj_weight.T, preferred_element_type=jnp.float32)
    return (grad_proj, grad_student, loss)
```

```python
import jax
import jax.numpy as jnp
from jax import lax
from jax.experimental import pallas as pl
from jax.experimental.pallas import tpu as pltpu
from jax.sharding import Mesh, PartitionSpec as P

D = 4096
grad_scale = 262144.0
f32, bf16 = jnp.float32, jnp.bfloat16

ROW = ("y", "core", "xl")
HALF = ("y", "xl")
PLANE = ("y", "core", "xh", "xl")
CHIPS = ("y", "xl", "xh")
NT = (((1,), (1,)), ((), ()))
TN = (((0,), (0,)), ((), ()))


def swap(value, axis):
    return lax.ppermute(value, axis, [(0, 1), (1, 0)])


def exchange(value, axes):
    return lax.all_to_all(value, axes, split_axis=0, concat_axis=0)


def share(value, axes, count):
    return exchange(jnp.broadcast_to(value[None], (count,) + value.shape), axes)


def ordered(index, own, other):
    first = index == 0
    return jnp.where(first, own, other), jnp.where(first, other, own)


def part_kernel(core_ref, hidden_ref, weight_ref, out_ref):
    both = jnp.concatenate([weight_ref[0], weight_ref[1]], axis=1)
    got = jnp.dot(hidden_ref[...], both, preferred_element_type=f32).astype(bf16)
    out_ref[0] = got[:, :128]
    out_ref[1] = got[:, 128:]


def parts_for(core, hidden, weight):
    tokens, depth = hidden.shape
    return pl.pallas_call(
        part_kernel,
        grid_spec=pltpu.PrefetchScalarGridSpec(
            num_scalar_prefetch=1,
            grid=(4,),
            in_specs=[
                pl.BlockSpec((tokens, depth), lambda i, c: (0, 0)),
                pl.BlockSpec((2, depth, 128), lambda i, c: (2 * i + c[0], 0, 0)),
            ],
            out_specs=pl.BlockSpec((2, tokens, 128), lambda i, c: (i, 0, 0)),
        ),
        out_shape=jax.ShapeDtypeStruct((8, tokens, 128), bf16),
        compiler_params=pltpu.CompilerParams(vmem_limit_bytes=32 << 20),
        cost_estimate=pl.CostEstimate(
            flops=2 * tokens * depth * 1024, bytes_accessed=5_000_000, transcendentals=0
        ),
    )(core.reshape(1).astype(jnp.int32), hidden, weight)


def on_device(
    hidden, residual, down_weight, norm_gain, seq_lengths, owner_slot, student_emb, proj_weight
):
    core, xh, z = lax.axis_index("core"), lax.axis_index("xh"), lax.axis_index("z")
    rank = lax.axis_index(ROW)
    root = jnp.sqrt(f32(D))
    low = xh == 0

    weight = lax.all_gather(down_weight, "z", axis=0)
    hidden2 = jnp.concatenate(ordered(xh, hidden, swap(hidden, "xh")), axis=0)

    left, right = residual[:, :128], residual[:, 128:]
    mine, theirs = jnp.where(low, left, right), jnp.where(low, right, left)
    table = jnp.pad(
        jnp.concatenate([seq_lengths, owner_slot], axis=1).astype(bf16), ((0, 15), (0, 64))
    )
    came = swap(jnp.concatenate([theirs, table], axis=0), "xh")
    residual2 = jnp.concatenate(ordered(xh, mine, came[:448]), axis=0)
    table2 = jnp.concatenate(ordered(xh, table[:1], came[448:449]), axis=0).astype(jnp.int32)
    lengths, owners = table2[:, :32], table2[:, 32:64]
    starts = jnp.cumsum(lengths, axis=1) - lengths
    places = jnp.arange(448, dtype=jnp.int32)
    inside = (places[None, None, :] >= starts[:, :, None]) & (
        places[None, None, :] < (starts + lengths)[:, :, None]
    )
    slot = jnp.arange(32, dtype=jnp.int32)
    slot = (slot % 16) * 2 + slot // 16
    select = (owners[:, None, :] == slot[None, :, None]).astype(bf16)
    member = jnp.einsum("bdi,bit->bdt", select, inside.astype(bf16), preferred_element_type=f32)
    empty = jnp.zeros((32, 448), f32)
    pool = jnp.stack(
        [
            jnp.concatenate([member[0], empty], axis=1),
            jnp.concatenate([empty, member[1]], axis=1),
        ],
        axis=1,
    ).reshape(64, 896)
    count = jnp.sum(pool, axis=1, keepdims=True)
    pool = pool.astype(bf16)

    piece = lax.dynamic_slice_in_dim(student_emb, 2 * rank, 2, axis=0)
    along = share(piece, "z", 16).reshape(32, 1024)
    plane = share(along, CHIPS, 16)
    even, odd = ordered(core, plane, swap(plane, "core"))
    emb = jnp.stack([even.reshape(4, 128, 1024), odd.reshape(4, 128, 1024)], axis=1).reshape(
        1024, 1024
    )
    u = jnp.dot(emb, proj_weight, preferred_element_type=f32)
    sum_uu = jnp.sum(share(jnp.sum(u * u, axis=1).reshape(8, 128), ROW, 16), axis=0).reshape(1024)
    scale_u = (1.0 / (root * jnp.sqrt(sum_uu / D + 1e-06)))[:, None]
    uhat = u * scale_u
    uhat_b = uhat.astype(bf16)
    uhat_own = jnp.where(low, uhat[:, :128], uhat[:, 128:])
    uhat_own_b = uhat_own.astype(bf16)
    gain = lax.dynamic_slice_in_dim(norm_gain, rank * 256 + xh * 128, 128)

    part_theirs = swap(parts_for(1 - core, hidden2, weight), "core")
    part_mine = parts_for(core, hidden2, weight)
    pair = (part_mine.astype(f32) + part_theirs.astype(f32)).astype(bf16)
    y = jnp.sum(exchange(pair, HALF).astype(f32), axis=0) + residual2.astype(f32)

    squares = jnp.sum(y * y, axis=1).reshape(7, 128)
    squares = jnp.sum(share(squares, PLANE, 32), axis=0).reshape(896)
    normed = (y * lax.rsqrt(squares / D + 1e-05)[:, None] * gain).astype(bf16)
    pooled = (jnp.dot(pool, normed, preferred_element_type=f32) / count).astype(bf16)

    tch = pooled.astype(f32)
    facing = lax.dynamic_slice_in_dim(uhat_own, z * 64, 64, axis=0)
    sums = jnp.concatenate([jnp.sum(tch * tch, axis=1), jnp.sum(tch * facing, axis=1)])
    sums = jnp.sum(share(sums.reshape(1, 128), PLANE, 32), axis=0).reshape(128)
    scale_t = 1.0 / (root * jnp.sqrt(sums[:64] / D + 1e-06))
    cosv = sums[64:] * scale_t
    cos_hi = cosv.astype(bf16)
    cos_lo = (cosv - cos_hi.astype(f32)).astype(bf16)
    that_b = (tch * scale_t[:, None]).astype(bf16)
    extra = jnp.pad(jnp.concatenate([cos_hi, cos_lo])[None], ((0, 15), (0, 0)))
    gathered = share(jnp.concatenate([that_b, extra], axis=0), "z", 16)
    teach = gathered[:, :64].reshape(1024, 128)
    cos_sum = jnp.sum(gathered[:, 64:65].astype(f32))
    teach2 = jnp.concatenate(ordered(xh, teach, swap(teach, "xh")), axis=1)

    lhs = jnp.concatenate([uhat_own_b, teach], axis=1)
    rhs = jnp.concatenate([uhat_own_b, -teach], axis=1)

    def rows_of(which):
        return lax.dot_general(
            lax.dynamic_slice_in_dim(lhs, which * 512, 512, axis=0),
            rhs,
            NT,
            preferred_element_type=f32,
        )

    diff_theirs = swap(rows_of(1 - core).astype(bf16), "core")
    diff_half = (rows_of(core) + diff_theirs.astype(f32)).astype(bf16)
    diff_rows = jnp.sum(exchange(diff_half.reshape(16, 32, 1024), CHIPS).astype(f32), axis=0)
    diff_own = share(diff_rows.astype(bf16), CHIPS, 16).reshape(512, 1024)
    diff_b = jnp.concatenate(ordered(core, diff_own, swap(diff_own, "core")), axis=0)
    diff_f = diff_b.astype(f32)
    loss = 1.0 - cos_sum / 1024 + jnp.sum(diff_f * diff_f) / 1024

    grad_hat = grad_scale * (
        -teach2.astype(f32) / 1024
        + 4.0 / 1024 * jnp.dot(diff_b, uhat_b, preferred_element_type=f32)
    )
    inner = jnp.sum(grad_hat * uhat, axis=1).reshape(8, 128)
    inner = jnp.sum(share(inner, ROW, 16), axis=0).reshape(1024, 1)
    du = ((grad_hat - uhat * inner) * scale_u).astype(bf16)
    grad_proj = lax.dot_general(emb, du, TN, preferred_element_type=f32)
    du_rows = lax.dynamic_index_in_dim(
        du.reshape(16, 32, 2, 256), xh * 16 + z, axis=1, keepdims=False
    ).reshape(32, 256)
    student = lax.dot_general(du_rows, proj_weight, NT, preferred_element_type=f32)
    student = student.astype(bf16)
    student = (student.astype(f32) + swap(student, "core").astype(f32)).astype(bf16)
    grad_student = jnp.sum(share(student, HALF, 8).astype(f32), axis=0)
    return (grad_proj, grad_student, loss)


def solution(mesh):
    fine = Mesh(mesh.devices.reshape(4, 2, 16, 2, 2), ("y", "core", "z", "xh", "xl"))
    dp = ("z", "xh")
    placed = (
        P(dp, ROW),
        P(dp, ROW),
        P(ROW, dp),
        P(),
        P(dp, None),
        P(dp, None),
        P(dp, None),
        P(None, ROW),
    )
    return jax.shard_map(
        on_device,
        mesh=fine,
        in_specs=placed,
        out_specs=(P(None, ROW), P(dp, None), P()),
        check_vma=False,
    )
```

```python
import jax
import jax.numpy as jnp
from jax import lax
from jax.experimental import pallas as pl
from jax.experimental.pallas import tpu as pltpu
from jax.sharding import Mesh, PartitionSpec as P

D = 4096
grad_scale = 262144.0
f32, bf16 = jnp.float32, jnp.bfloat16

ROW = ("y", "core", "xl")
HALF = ("y", "xl")
PLANE = ("y", "core", "xh", "xl")
CHIPS = ("y", "xl", "xh")
NT = (((1,), (1,)), ((), ()))
TN = (((0,), (0,)), ((), ()))


def swap(value, axis):
    return lax.ppermute(value, axis, [(0, 1), (1, 0)])


def exchange(value, axes):
    return lax.all_to_all(value, axes, split_axis=0, concat_axis=0)


def share(value, axes, count):
    return exchange(jnp.broadcast_to(value[None], (count,) + value.shape), axes)


def two_parts(value):
    high = lax.reduce_precision(value, 8, 7)
    return high.astype(bf16), (value - high).astype(bf16)


def ordered(index, own, other):
    first = index == 0
    return jnp.where(first, own, other), jnp.where(first, other, own)


def part_kernel(core_ref, hidden_ref, weight_ref, out_ref):
    both = jnp.concatenate([weight_ref[0], weight_ref[1]], axis=1)
    got = jnp.dot(hidden_ref[...], both, preferred_element_type=f32).astype(bf16)
    out_ref[0] = got[:, :128]
    out_ref[1] = got[:, 128:]


def parts_for(core, hidden, weight):
    tokens, depth = hidden.shape
    return pl.pallas_call(
        part_kernel,
        grid_spec=pltpu.PrefetchScalarGridSpec(
            num_scalar_prefetch=1,
            grid=(4,),
            in_specs=[
                pl.BlockSpec((tokens, depth), lambda i, c: (0, 0)),
                pl.BlockSpec((2, depth, 128), lambda i, c: (2 * i + c[0], 0, 0)),
            ],
            out_specs=pl.BlockSpec((2, tokens, 128), lambda i, c: (i, 0, 0)),
        ),
        out_shape=jax.ShapeDtypeStruct((8, tokens, 128), bf16),
        compiler_params=pltpu.CompilerParams(vmem_limit_bytes=32 << 20),
        cost_estimate=pl.CostEstimate(
            flops=2 * tokens * depth * 1024, bytes_accessed=5_000_000, transcendentals=0
        ),
    )(core.reshape(1).astype(jnp.int32), hidden, weight)


def on_device(
    hidden, residual, down_weight, norm_gain, seq_lengths, owner_slot, student_emb, proj_weight
):
    core, xh, z = lax.axis_index("core"), lax.axis_index("xh"), lax.axis_index("z")
    rank = lax.axis_index(ROW)
    root = jnp.sqrt(f32(D))
    low = xh == 0

    weight = lax.all_gather(down_weight, "z", axis=0)
    left, right = residual[:, :128], residual[:, 128:]
    mine, theirs = jnp.where(low, left, right), jnp.where(low, right, left)
    table = jnp.pad(
        jnp.concatenate([seq_lengths, owner_slot], axis=1).astype(bf16), ((0, 15), (0, 64))
    )
    came = swap(jnp.concatenate([theirs, table], axis=0), "xh")
    residual2 = jnp.concatenate(ordered(xh, mine, came[:448]), axis=0)
    table2 = jnp.concatenate(ordered(xh, table[:1], came[448:449]), axis=0).astype(jnp.int32)
    lengths, owners = table2[:, :32], table2[:, 32:64]
    starts = jnp.cumsum(lengths, axis=1) - lengths
    places = jnp.arange(448, dtype=jnp.int32)
    inside = (places[None, None, :] >= starts[:, :, None]) & (
        places[None, None, :] < (starts + lengths)[:, :, None]
    )
    slot = jnp.arange(32, dtype=jnp.int32)
    slot = (slot % 16) * 2 + slot // 16
    select = (owners[:, None, :] == slot[None, :, None]).astype(bf16)
    member = jnp.einsum("bdi,bit->bdt", select, inside.astype(bf16), preferred_element_type=f32)
    empty = jnp.zeros((32, 448), f32)
    pool = jnp.stack(
        [
            jnp.concatenate([member[0], empty], axis=1),
            jnp.concatenate([empty, member[1]], axis=1),
        ],
        axis=1,
    ).reshape(64, 896)
    count = jnp.sum(pool, axis=1, keepdims=True)
    pool = pool.astype(bf16)

    piece = lax.dynamic_slice_in_dim(student_emb, 2 * rank, 2, axis=0)
    along = share(piece, "z", 16).reshape(32, 1024)
    along, hidden, pool, count, residual2 = lax.optimization_barrier(
        (along, hidden, pool, count, residual2)
    )
    hidden2 = jnp.concatenate(ordered(xh, hidden, swap(hidden, "xh")), axis=0)
    plane = share(along, CHIPS, 16)
    even, odd = ordered(core, plane, swap(plane, "core"))
    emb = jnp.stack([even.reshape(4, 128, 1024), odd.reshape(4, 128, 1024)], axis=1).reshape(
        1024, 1024
    )
    u = jnp.dot(emb, proj_weight, preferred_element_type=f32)
    sum_uu = jnp.sum(share(jnp.sum(u * u, axis=1).reshape(8, 128), ROW, 16), axis=0).reshape(1024)
    inverse_u = 1.0 / (root * jnp.sqrt(sum_uu / D + 1e-06))
    scale_u = inverse_u[:, None]
    uhat = u * scale_u
    uhat_b = uhat.astype(bf16)
    uhat_own = jnp.where(low, uhat[:, :128], uhat[:, 128:])
    proj_own = jnp.where(low, proj_weight[:, :128], proj_weight[:, 128:])
    gain = lax.dynamic_slice_in_dim(norm_gain, rank * 256 + xh * 128, 128)
    pick = jnp.arange(1024, dtype=jnp.int32)
    chosen = (pick // 64 * 2 + pick % 2)[None, :] == jnp.arange(32, dtype=jnp.int32)[:, None]
    student_of = (pick // 2 % 32)[None, :]
    chosen2 = jnp.concatenate([chosen & (student_of == z), chosen & (student_of == 16 + z)]).astype(bf16)
    chosen = (chosen & (student_of == xh * 16 + z)).astype(bf16)
    image = lax.dot_general(uhat_b, proj_weight, NT, preferred_element_type=f32).astype(bf16)

    hidden2, uhat, image = lax.optimization_barrier(
        (hidden2, uhat, image)
    )
    image = lax.all_gather(
        lax.psum_scatter(image, ROW, scatter_dimension=0, tiled=True), ROW, axis=0, tiled=True
    )

    part_theirs = swap(parts_for(1 - core, hidden2, weight), "core")
    part_mine = parts_for(core, hidden2, weight)
    pair = (part_mine.astype(f32) + part_theirs.astype(f32)).astype(bf16)
    y = jnp.sum(exchange(pair, HALF).astype(f32), axis=0) + residual2.astype(f32)

    squares = jnp.sum(y * y, axis=1).reshape(7, 128)
    squares = jnp.sum(share(squares, PLANE, 32), axis=0).reshape(896)
    normed = (y * lax.rsqrt(squares / D + 1e-05)[:, None] * gain).astype(bf16)
    pooled = (jnp.dot(pool, normed, preferred_element_type=f32) / count).astype(bf16)
    teach = share(pooled, "z", 16).reshape(1024, 128)
    teach_other = swap(teach, "xh")

    def rows_of(which):
        return lax.dot_general(
            lax.dynamic_slice_in_dim(teach, which * 512, 512, axis=0),
            teach,
            NT,
            preferred_element_type=f32,
        ).astype(bf16)

    tch = teach.astype(f32)
    sum_tt = jnp.sum(tch * tch, axis=1)
    cross = jnp.sum(tch * uhat_own, axis=1).astype(bf16)
    tt_hi, tt_lo = two_parts(sum_tt)
    teach_d = jnp.dot(chosen2, teach, preferred_element_type=f32).astype(bf16)
    image_t = lax.dot_general(teach_d, proj_own, NT, preferred_element_type=f32).astype(bf16)
    image_l, image_r = image_t[:, :512].reshape(32, 1024), image_t[:, 512:].reshape(32, 1024)
    even_core = core == 0
    sums = jnp.stack([tt_hi, tt_lo, cross])

    def packet(which, image_half):
        return jnp.concatenate([rows_of(which), image_half, jnp.pad(sums, ((0, 5), (0, 0)))])

    came = swap(packet(1 - core, jnp.where(even_core, image_r, image_l)), "core")
    own = packet(core, jnp.where(even_core, image_l, image_r))
    both = own.astype(f32) + came.astype(f32)
    tt_hi, tt_lo = two_parts(both[544] + both[545])
    sums = jnp.stack([tt_hi, tt_lo, both[546].astype(bf16)])
    pair = jnp.concatenate(
        [
            both[:512].astype(bf16).reshape(16, 32, 1024),
            jnp.broadcast_to(sums[None], (16, 3, 1024)),
            both[512:544].astype(bf16).reshape(16, 2, 1024),
            jnp.zeros((16, 3, 1024), bf16),
        ],
        axis=1,
    )
    total = jnp.sum(exchange(pair, CHIPS).astype(f32), axis=0)
    sum_tt = total[32] + total[33]
    scale_t = 1.0 / (root * jnp.sqrt(sum_tt / D + 1e-06))
    cosv = total[34] * scale_t
    first = core * 512 + lax.axis_index(CHIPS) * 32
    gram_u = inverse_u[None, :] * lax.dot_general(
        lax.dynamic_slice_in_dim(image, first, 32, axis=0), emb, NT, preferred_element_type=f32
    )
    scale_rows = lax.dynamic_slice_in_dim(scale_t, first, 32)
    diff = (gram_u - total[:32] * scale_t[None, :] * scale_rows[:, None]).astype(bf16)
    inner = 4.0 * jnp.sum(diff.astype(f32) * gram_u, axis=1) - lax.dynamic_slice_in_dim(
        cosv, first, 32
    )
    in_hi, in_lo = two_parts(inner)
    block = jnp.concatenate(
        [
            diff,
            total[35:37].astype(bf16),
            jnp.pad(jnp.concatenate([in_hi, in_lo])[None], ((0, 5), (0, 960))),
        ]
    )
    block = share(block, CHIPS, 16)
    even, odd = ordered(core, block, swap(block, "core"))
    diff_b = jnp.concatenate([even[:, :32].reshape(512, 1024), odd[:, :32].reshape(512, 1024)])
    near = lax.dynamic_slice_in_dim(even, xh * 8, 8)[:, 32:34].reshape(32, 512)
    far = lax.dynamic_slice_in_dim(odd, xh * 8, 8)[:, 32:34].reshape(32, 512)
    image_t = jnp.concatenate([near, far], axis=1)
    in_hi = jnp.concatenate([even[:, 34, :32], odd[:, 34, :32]]).reshape(1024)
    in_lo = jnp.concatenate([even[:, 34, 32:64], odd[:, 34, 32:64]]).reshape(1024)
    inner = in_hi.astype(f32) + in_lo.astype(f32)
    diff_b, teach_other = lax.optimization_barrier((diff_b, teach_other))
    teach2 = jnp.concatenate(ordered(xh, teach, teach_other), axis=1)
    diff_f = diff_b.astype(f32)
    loss = 1.0 - jnp.sum(cosv) / 1024 + jnp.sum(diff_f * diff_f) / 1024

    grad_hat = 4.0 * jnp.dot(diff_b, uhat_b, preferred_element_type=f32) - (
        teach2.astype(f32) * scale_t[:, None]
    )
    du = (grad_hat - uhat * inner[:, None]) * scale_u
    du = (du * (grad_scale / 1024)).astype(bf16)
    grad_proj = lax.dot_general(emb, du, TN, preferred_element_type=f32)

    mask = chosen.astype(f32)
    scale_t_d = jnp.sum(mask * scale_t[None, :], axis=1, keepdims=True)
    scale_u_d = jnp.sum(mask * inverse_u[None, :], axis=1, keepdims=True)
    inner_d = jnp.sum(mask * inner[None, :], axis=1, keepdims=True)
    diff_d = jnp.dot(chosen, diff_b, preferred_element_type=f32).astype(bf16)
    image_d = jnp.dot(chosen, image, preferred_element_type=f32)
    student = (
        4.0 * jnp.dot(diff_d, image, preferred_element_type=f32)
        - scale_t_d * image_t.astype(f32)
        - inner_d * image_d
    )
    grad_student = student * scale_u_d * (grad_scale / 1024)
    return (grad_proj, grad_student, loss)


def solution(mesh):
    fine = Mesh(mesh.devices.reshape(4, 2, 16, 2, 2), ("y", "core", "z", "xh", "xl"))
    dp = ("z", "xh")
    placed = (
        P(dp, ROW),
        P(dp, ROW),
        P(ROW, dp),
        P(),
        P(dp, None),
        P(dp, None),
        P(dp, None),
        P(None, ROW),
    )
    return jax.shard_map(
        on_device,
        mesh=fine,
        in_specs=placed,
        out_specs=(P(None, ROW), P(dp, None), P()),
        check_vma=False,
    )
```

```python
import jax
import jax.numpy as jnp
from jax import lax
from jax.experimental import pallas as pl
from jax.experimental.pallas import tpu as pltpu
from jax.sharding import Mesh, PartitionSpec as P

D = 4096
grad_scale = 262144.0
f32, bf16 = jnp.float32, jnp.bfloat16

ROW = ("y", "core", "xl")
HALF = ("y", "xl")
PLANE = ("y", "core", "xh", "xl")
CHIPS = ("y", "xl", "xh")
NT = (((1,), (1,)), ((), ()))
TN = (((0,), (0,)), ((), ()))


def swap(value, axis):
    return lax.ppermute(value, axis, [(0, 1), (1, 0)])


def exchange(value, axes):
    return lax.all_to_all(value, axes, split_axis=0, concat_axis=0)


def share(value, axes, count):
    return exchange(jnp.broadcast_to(value[None], (count,) + value.shape), axes)


def two_parts(value):
    high = lax.reduce_precision(value, 8, 7)
    return high.astype(bf16), (value - high).astype(bf16)


def ordered(index, own, other):
    first = index == 0
    return jnp.where(first, own, other), jnp.where(first, other, own)


def part_kernel(core_ref, hidden_ref, weight_ref, out_ref):
    both = jnp.concatenate([weight_ref[0], weight_ref[1]], axis=1)
    got = jnp.dot(hidden_ref[...], both, preferred_element_type=f32).astype(bf16)
    out_ref[0] = got[:, :128]
    out_ref[1] = got[:, 128:]


def parts_for(core, hidden, weight):
    tokens, depth = hidden.shape
    assert weight.shape[1] >= depth
    return pl.pallas_call(
        part_kernel,
        grid_spec=pltpu.PrefetchScalarGridSpec(
            num_scalar_prefetch=1,
            grid=(4,),
            in_specs=[
                pl.BlockSpec((tokens, depth), lambda i, c: (0, 0)),
                pl.BlockSpec((2, depth, 128), lambda i, c: (2 * i + c[0], 0, 0)),
            ],
            out_specs=pl.BlockSpec((2, tokens, 128), lambda i, c: (i, 0, 0)),
        ),
        out_shape=jax.ShapeDtypeStruct((8, tokens, 128), bf16),
        compiler_params=pltpu.CompilerParams(vmem_limit_bytes=32 << 20),
        cost_estimate=pl.CostEstimate(
            flops=2 * tokens * depth * 1024, bytes_accessed=5_000_000, transcendentals=0
        ),
    )(core.reshape(1).astype(jnp.int32), hidden, weight)


def on_device(
    hidden, residual, down_weight, norm_gain, seq_lengths, owner_slot, student_emb, proj_weight
):
    core, xh, z = lax.axis_index("core"), lax.axis_index("xh"), lax.axis_index("z")
    rank = lax.axis_index(ROW)
    root = jnp.sqrt(f32(D))
    low = xh == 0

    slabs = student_emb.reshape(32, 8, 128).transpose(1, 0, 2).reshape(256, 128)
    weight = lax.all_gather(jnp.concatenate([down_weight, slabs]), "z", axis=0)

    left, right = residual[:, :128], residual[:, 128:]
    mine, theirs = jnp.where(low, left, right), jnp.where(low, right, left)
    table = jnp.pad(
        jnp.concatenate([seq_lengths, owner_slot], axis=1).astype(bf16), ((0, 15), (0, 64))
    )
    came = swap(jnp.concatenate([theirs, table], axis=0), "xh")
    residual2 = jnp.concatenate(ordered(xh, mine, came[:448]), axis=0)
    table2 = jnp.concatenate(ordered(xh, table[:1], came[448:449]), axis=0).astype(jnp.int32)
    lengths, owners = table2[:, :32], table2[:, 32:64]
    starts = jnp.cumsum(lengths, axis=1) - lengths
    places = jnp.arange(448, dtype=jnp.int32)
    inside = (places[None, None, :] >= starts[:, :, None]) & (
        places[None, None, :] < (starts + lengths)[:, :, None]
    )
    slot = jnp.arange(32, dtype=jnp.int32)
    slot = (slot % 16) * 2 + slot // 16
    select = (owners[:, None, :] == slot[None, :, None]).astype(bf16)
    member = jnp.einsum("bdi,bit->bdt", select, inside.astype(bf16), preferred_element_type=f32)
    empty = jnp.zeros((32, 448), f32)
    pool = jnp.stack(
        [
            jnp.concatenate([member[0], empty], axis=1),
            jnp.concatenate([empty, member[1]], axis=1),
        ],
        axis=1,
    ).reshape(64, 896)
    count = jnp.sum(pool, axis=1, keepdims=True)
    pool = pool.astype(bf16)

    def product_rows(which):
        return lax.dot_general(
            lax.dynamic_slice_in_dim(proj_weight, which * 512, 512, axis=0),
            proj_weight,
            NT,
            preferred_element_type=f32,
        ).astype(bf16)

    product = swap(product_rows(1 - core), "core").astype(f32)
    product = (product + product_rows(core).astype(f32)).astype(bf16)
    product, hidden, pool, count, residual2 = lax.optimization_barrier(
        (product, hidden, pool, count, residual2)
    )
    hidden2 = jnp.concatenate(ordered(xh, hidden, swap(hidden, "xh")), axis=0)
    product = jnp.sum(exchange(product.reshape(8, 64, 1024), HALF).astype(f32), axis=0)
    product = share(product.astype(bf16), HALF, 8).reshape(512, 1024)
    product = jnp.concatenate(ordered(core, product, swap(product, "core")))
    hidden2, product = lax.optimization_barrier((hidden2, product))

    proj_own = jnp.where(low, proj_weight[:, :128], proj_weight[:, 128:])
    gain = lax.dynamic_slice_in_dim(norm_gain, rank * 256 + xh * 128, 128)
    pick = jnp.arange(1024, dtype=jnp.int32)
    place = pick // 2 % 32
    chosen = (pick // 64 * 2 + pick % 2)[None, :] == jnp.arange(32, dtype=jnp.int32)[:, None]
    student_of = place[None, :]
    source = place * 32 + pick // 64 * 2 + pick % 2
    order = (source[:, None] == pick[None, :]).astype(bf16)
    chosen2 = jnp.concatenate([chosen & (student_of == z), chosen & (student_of == 16 + z)]).astype(bf16)
    chosen = (chosen & (student_of == xh * 16 + z)).astype(bf16)

    part_theirs = swap(parts_for(1 - core, hidden2, weight), "core")
    part_mine = parts_for(core, hidden2, weight)
    pair = (part_mine.astype(f32) + part_theirs.astype(f32)).astype(bf16)
    y = jnp.sum(exchange(pair, HALF).astype(f32), axis=0) + residual2.astype(f32)

    squares = jnp.sum(y * y, axis=1).reshape(7, 128)
    squares = jnp.sum(share(squares, PLANE, 32), axis=0).reshape(896)
    squares, slabs = lax.optimization_barrier((squares, weight[:, 896:]))
    far = swap(lax.dynamic_slice_in_dim(slabs, core * 8, 8), "xh")
    far = jnp.concatenate(ordered(core, far, swap(far, "core")))
    emb = jnp.concatenate(ordered(xh, slabs, far)).reshape(32, 8, 32, 128)
    emb = emb.transpose(0, 2, 1, 3).reshape(1024, 1024)
    normed = (y * lax.rsqrt(squares / D + 1e-05)[:, None] * gain).astype(bf16)
    pooled = (jnp.dot(pool, normed, preferred_element_type=f32) / count).astype(bf16)
    teach = share(pooled, "z", 16).reshape(1024, 128)
    teach_other = swap(teach, "xh")

    emb = jnp.dot(order, emb, preferred_element_type=f32).astype(bf16)
    u = jnp.dot(emb, proj_weight, preferred_element_type=f32)
    u_own = jnp.where(low, u[:, :128], u[:, 128:])
    uu_hi, uu_lo = two_parts(jnp.sum(u_own * u_own, axis=1))
    first = core * 512 + lax.axis_index(CHIPS) * 32
    gram_raw = lax.dot_general(
        jnp.dot(
            lax.dynamic_slice_in_dim(emb, first, 32), product, preferred_element_type=f32
        ).astype(bf16),
        emb,
        NT,
        preferred_element_type=f32,
    )
    image_d = jnp.dot(student_emb, product, preferred_element_type=f32)

    def rows_of(which):
        return lax.dot_general(
            lax.dynamic_slice_in_dim(teach, which * 512, 512, axis=0),
            teach,
            NT,
            preferred_element_type=f32,
        ).astype(bf16)

    tch = teach.astype(f32)
    sum_tt = jnp.sum(tch * tch, axis=1)
    cross = jnp.sum(tch * u_own, axis=1).astype(bf16)
    tt_hi, tt_lo = two_parts(sum_tt)
    teach_d = jnp.dot(chosen2, teach, preferred_element_type=f32).astype(bf16)
    image_t = lax.dot_general(teach_d, proj_own, NT, preferred_element_type=f32).astype(bf16)
    image_l, image_r = image_t[:, :512].reshape(32, 1024), image_t[:, 512:].reshape(32, 1024)
    even_core = core == 0
    sums = jnp.stack([tt_hi, tt_lo, uu_hi, uu_lo, cross])

    def packet(which, image_half):
        return jnp.concatenate([rows_of(which), image_half, jnp.pad(sums, ((0, 3), (0, 0)))])

    came = swap(packet(1 - core, jnp.where(even_core, image_r, image_l)), "core")
    own = packet(core, jnp.where(even_core, image_l, image_r))
    both = own.astype(f32) + came.astype(f32)
    tt_hi, tt_lo = two_parts(both[544] + both[545])
    uu_hi, uu_lo = two_parts(both[546] + both[547])
    sums = jnp.stack([tt_hi, tt_lo, uu_hi, uu_lo, both[548].astype(bf16)])
    pair = jnp.concatenate(
        [
            both[:512].astype(bf16).reshape(16, 32, 1024),
            jnp.broadcast_to(sums[None], (16, 5, 1024)),
            both[512:544].astype(bf16).reshape(16, 2, 1024),
            jnp.zeros((16, 1, 1024), bf16),
        ],
        axis=1,
    )
    total = jnp.sum(exchange(pair, CHIPS).astype(f32), axis=0)
    total, teach_other = lax.optimization_barrier((total, teach_other))
    sum_tt = total[32] + total[33]
    scale_t = 1.0 / (root * jnp.sqrt(sum_tt / D + 1e-06))
    inverse_u = 1.0 / (root * jnp.sqrt((total[34] + total[35]) / D + 1e-06))
    scale_u = inverse_u[:, None]
    uhat = u * scale_u
    uhat_b = uhat.astype(bf16)
    cosv = total[36] * scale_t * inverse_u
    gram_u = gram_raw * inverse_u[None, :] * lax.dynamic_slice_in_dim(inverse_u, first, 32)[:, None]
    scale_rows = lax.dynamic_slice_in_dim(scale_t, first, 32)
    diff = (gram_u - total[:32] * scale_t[None, :] * scale_rows[:, None]).astype(bf16)
    inner = 4.0 * jnp.sum(diff.astype(f32) * gram_u, axis=1) - lax.dynamic_slice_in_dim(
        cosv, first, 32
    )
    in_hi, in_lo = two_parts(inner)
    block = jnp.concatenate(
        [
            diff,
            total[37:39].astype(bf16),
            jnp.pad(jnp.concatenate([in_hi, in_lo])[None], ((0, 5), (0, 960))),
        ]
    )
    block = share(block, CHIPS, 16)
    even, odd = ordered(core, block, swap(block, "core"))
    diff_b = jnp.concatenate([even[:, :32].reshape(512, 1024), odd[:, :32].reshape(512, 1024)])
    near = lax.dynamic_slice_in_dim(even, xh * 8, 8)[:, 32:34].reshape(32, 512)
    far = lax.dynamic_slice_in_dim(odd, xh * 8, 8)[:, 32:34].reshape(32, 512)
    image_t = jnp.concatenate([near, far], axis=1)
    in_hi = jnp.concatenate([even[:, 34, :32], odd[:, 34, :32]]).reshape(1024)
    in_lo = jnp.concatenate([even[:, 34, 32:64], odd[:, 34, 32:64]]).reshape(1024)
    inner = in_hi.astype(f32) + in_lo.astype(f32)
    teach2 = jnp.concatenate(ordered(xh, teach, teach_other), axis=1)
    diff_f = diff_b.astype(f32)
    loss = 1.0 - jnp.sum(cosv) / 1024 + jnp.sum(diff_f * diff_f) / 1024

    grad_hat = 4.0 * jnp.dot(diff_b, uhat_b, preferred_element_type=f32) - (
        teach2.astype(f32) * scale_t[:, None]
    )
    du = (grad_hat - uhat * inner[:, None]) * scale_u
    du = (du * (grad_scale / 1024)).astype(bf16)
    grad_proj = lax.dot_general(emb, du, TN, preferred_element_type=f32)

    mask = chosen.astype(f32)
    scale_t_d = jnp.sum(mask * scale_t[None, :], axis=1, keepdims=True)
    scale_u_d = jnp.sum(mask * inverse_u[None, :], axis=1, keepdims=True)
    inner_d = jnp.sum(mask * inner[None, :], axis=1, keepdims=True)
    diff_d = jnp.dot(chosen, diff_b, preferred_element_type=f32) * inverse_u[None, :]
    mixed = jnp.dot(diff_d.astype(bf16), emb, preferred_element_type=f32).astype(bf16)
    student = (
        4.0 * jnp.dot(mixed, product, preferred_element_type=f32)
        - scale_t_d * image_t.astype(f32)
        - inner_d * scale_u_d * image_d
    )
    grad_student = student * scale_u_d * (grad_scale / 1024)
    return (grad_proj, grad_student, loss)


def solution(mesh):
    fine = Mesh(mesh.devices.reshape(4, 2, 16, 2, 2), ("y", "core", "z", "xh", "xl"))
    dp = ("z", "xh")
    placed = (
        P(dp, ROW),
        P(dp, ROW),
        P(ROW, dp),
        P(),
        P(dp, None),
        P(dp, None),
        P(dp, None),
        P(None, ROW),
    )
    return jax.shard_map(
        on_device,
        mesh=fine,
        in_specs=placed,
        out_specs=(P(None, ROW), P(dp, None), P()),
        check_vma=False,
    )
```

```python
import jax
import jax.numpy as jnp
from jax import lax
from jax.experimental import pallas as pl
from jax.experimental.pallas import tpu as pltpu
from jax.sharding import Mesh, PartitionSpec as P

D = 4096
grad_scale = 262144.0
f32, bf16 = jnp.float32, jnp.bfloat16

ROW = ("y", "core", "xl")
HALF = ("y", "xl")
PLANE = ("y", "core", "xh", "xl")
CHIPS = ("y", "xl", "xh")
NT = (((1,), (1,)), ((), ()))


def swap(value, axis):
    return lax.ppermute(value, axis, [(0, 1), (1, 0)])


def exchange(value, axes):
    return lax.all_to_all(value, axes, split_axis=0, concat_axis=0)


def share(value, axes, count):
    return exchange(jnp.broadcast_to(value[None], (count,) + value.shape), axes)


def two_parts(value):
    high = lax.reduce_precision(value, 8, 7)
    return high.astype(bf16), (value - high).astype(bf16)


def ordered(index, own, other):
    first = index == 0
    return jnp.where(first, own, other), jnp.where(first, other, own)


def part_kernel(core_ref, hidden_ref, weight_ref, weight_b_ref, out_ref):
    both = jnp.concatenate([weight_ref[0], weight_ref[1]], axis=1)
    got = jnp.dot(hidden_ref[:, :512], both, preferred_element_type=f32)
    both = jnp.concatenate([weight_b_ref[0], weight_b_ref[1]], axis=1)
    got = got + jnp.dot(hidden_ref[:, 512:], both, preferred_element_type=f32)
    got = got.astype(bf16)
    out_ref[0] = got[:, :128]
    out_ref[1] = got[:, 128:]


def parts_for(core, hidden, weight, weight_b):
    tokens, depth = hidden.shape
    return pl.pallas_call(
        part_kernel,
        grid_spec=pltpu.PrefetchScalarGridSpec(
            num_scalar_prefetch=1,
            grid=(4,),
            in_specs=[
                pl.BlockSpec((tokens, depth), lambda i, c: (0, 0)),
                pl.BlockSpec((2, 512, 128), lambda i, c: (2 * i + c[0], 0, 0)),
                pl.BlockSpec((2, depth - 512, 128), lambda i, c: (2 * i + c[0], 0, 0)),
            ],
            out_specs=pl.BlockSpec((2, tokens, 128), lambda i, c: (i, 0, 0)),
        ),
        out_shape=jax.ShapeDtypeStruct((8, tokens, 128), bf16),
        compiler_params=pltpu.CompilerParams(vmem_limit_bytes=32 << 20),
        cost_estimate=pl.CostEstimate(
            flops=2 * tokens * depth * 1024, bytes_accessed=5_000_000, transcendentals=0
        ),
    )(core.reshape(1).astype(jnp.int32), hidden, weight, weight_b)


def on_device(
    hidden, residual, down_weight, norm_gain, seq_lengths, owner_slot, student_emb, proj_weight
):
    core, xh, z = lax.axis_index("core"), lax.axis_index("xh"), lax.axis_index("z")
    rank = lax.axis_index(ROW)
    root = jnp.sqrt(f32(D))
    low = xh == 0

    slabs = student_emb.reshape(32, 8, 128).transpose(1, 0, 2).reshape(256, 128)
    weight = lax.all_gather(down_weight[:512], "z", axis=0)
    weight_b = lax.all_gather(jnp.concatenate([down_weight[512:], slabs]), "z", axis=0)

    left, right = residual[:, :128], residual[:, 128:]
    mine, theirs = jnp.where(low, left, right), jnp.where(low, right, left)
    table = jnp.pad(
        jnp.concatenate([seq_lengths, owner_slot], axis=1).astype(bf16), ((0, 15), (0, 64))
    )
    came = swap(jnp.concatenate([theirs, table], axis=0), "xh")
    residual2 = jnp.concatenate(ordered(xh, mine, came[:448]), axis=0)
    table2 = jnp.concatenate(ordered(xh, table[:1], came[448:449]), axis=0).astype(jnp.int32)
    lengths, owners = table2[:, :32], table2[:, 32:64]
    starts = jnp.cumsum(lengths, axis=1) - lengths
    places = jnp.arange(448, dtype=jnp.int32)
    inside = (places[None, None, :] >= starts[:, :, None]) & (
        places[None, None, :] < (starts + lengths)[:, :, None]
    )
    slot = jnp.arange(32, dtype=jnp.int32)
    slot = (slot % 16) * 2 + slot // 16
    select = (owners[:, None, :] == slot[None, :, None]).astype(bf16)
    member = jnp.einsum("bdi,bit->bdt", select, inside.astype(bf16), preferred_element_type=f32)
    empty = jnp.zeros((32, 448), f32)
    pool = jnp.stack(
        [
            jnp.concatenate([member[0], empty], axis=1),
            jnp.concatenate([empty, member[1]], axis=1),
        ],
        axis=1,
    ).reshape(64, 896)
    count = jnp.sum(pool, axis=1, keepdims=True)
    pool = pool.astype(bf16)

    def product_rows(which):
        return lax.dot_general(
            lax.dynamic_slice_in_dim(proj_weight, which * 512, 512, axis=0),
            proj_weight,
            NT,
            preferred_element_type=f32,
        ).astype(bf16)

    product = swap(product_rows(1 - core), "core").astype(f32)
    product = (product + product_rows(core).astype(f32)).astype(bf16)
    product, hidden, pool, count, residual2 = lax.optimization_barrier(
        (product, hidden, pool, count, residual2)
    )
    hidden2 = jnp.concatenate(ordered(xh, hidden, swap(hidden, "xh")), axis=0)
    product = jnp.sum(exchange(product.reshape(8, 64, 1024), HALF).astype(f32), axis=0)
    product = share(product.astype(bf16), HALF, 8).reshape(512, 1024)
    product = jnp.concatenate(ordered(core, product, swap(product, "core")))
    hidden2, product = lax.optimization_barrier((hidden2, product))

    proj_own = jnp.where(low, proj_weight[:, :128], proj_weight[:, 128:])
    gain = lax.dynamic_slice_in_dim(norm_gain, rank * 256 + xh * 128, 128)
    pick = jnp.arange(1024, dtype=jnp.int32)
    place = pick // 2 % 32
    chosen = (pick // 64 * 2 + pick % 2)[None, :] == jnp.arange(32, dtype=jnp.int32)[:, None]
    student_of = place[None, :]
    source = place * 32 + pick // 64 * 2 + pick % 2
    order = (source[:, None] == pick[None, :]).astype(bf16)
    chosen2 = jnp.concatenate([chosen & (student_of == z), chosen & (student_of == 16 + z)]).astype(bf16)
    chosen = (chosen & (student_of == xh * 16 + z)).astype(bf16)

    slabs = weight_b[:, 384:]
    far = swap(lax.dynamic_slice_in_dim(slabs, core * 8, 8), "xh")
    part_theirs = swap(parts_for(1 - core, hidden2, weight, weight_b), "core")
    part_mine = parts_for(core, hidden2, weight, weight_b)
    pair = (part_mine.astype(f32) + part_theirs.astype(f32)).astype(bf16)
    y = jnp.sum(exchange(pair, HALF).astype(f32), axis=0) + residual2.astype(f32)

    y, far = lax.optimization_barrier((y, far))
    squares = jnp.sum(y * y, axis=1).reshape(7, 128)
    squares = jnp.sum(share(squares, PLANE, 32), axis=0).reshape(896)
    far = jnp.concatenate(ordered(core, far, swap(far, "core")))
    squares, far = lax.optimization_barrier((squares, far))
    emb = jnp.concatenate(ordered(xh, slabs, far)).reshape(32, 8, 32, 128)
    emb = emb.transpose(0, 2, 1, 3).reshape(1024, 1024)
    normed = (y * lax.rsqrt(squares / D + 1e-05)[:, None] * gain).astype(bf16)
    pooled = (jnp.dot(pool, normed, preferred_element_type=f32) / count).astype(bf16)
    teach = share(pooled, "z", 16).reshape(1024, 128)
    teach_other = swap(teach, "xh")

    emb_t = lax.dot_general(emb, order, (((0,), (1,)), ((), ())), preferred_element_type=f32)
    emb_t = emb_t.astype(bf16)
    emb = jnp.dot(order, emb, preferred_element_type=f32).astype(bf16)
    u = jnp.dot(emb, proj_weight, preferred_element_type=f32)
    u_own = jnp.where(low, u[:, :128], u[:, 128:])
    uu_hi, uu_lo = two_parts(jnp.sum(u_own * u_own, axis=1))
    first = core * 512 + lax.axis_index(CHIPS) * 32
    gram_raw = lax.dot_general(
        jnp.dot(
            lax.dynamic_slice_in_dim(emb, first, 32), product, preferred_element_type=f32
        ).astype(bf16),
        emb,
        NT,
        preferred_element_type=f32,
    )
    image_d = jnp.dot(student_emb, product, preferred_element_type=f32)

    def rows_of(which):
        return lax.dot_general(
            lax.dynamic_slice_in_dim(teach, which * 512, 512, axis=0),
            teach,
            NT,
            preferred_element_type=f32,
        ).astype(bf16)

    tch = teach.astype(f32)
    sum_tt = jnp.sum(tch * tch, axis=1)
    cross = jnp.sum(tch * u_own, axis=1).astype(bf16)
    tt_hi, tt_lo = two_parts(sum_tt)
    teach_d = jnp.dot(chosen2, teach, preferred_element_type=f32).astype(bf16)
    image_t = lax.dot_general(teach_d, proj_own, NT, preferred_element_type=f32).astype(bf16)
    image_l, image_r = image_t[:, :512].reshape(32, 1024), image_t[:, 512:].reshape(32, 1024)
    even_core = core == 0
    sums = jnp.stack([tt_hi, tt_lo, uu_hi, uu_lo, cross])

    def packet(which, image_half):
        return jnp.concatenate([rows_of(which), image_half, jnp.pad(sums, ((0, 3), (0, 0)))])

    going, teach_other = lax.optimization_barrier(
        (packet(1 - core, jnp.where(even_core, image_r, image_l)), teach_other)
    )
    came = swap(going, "core")
    own = packet(core, jnp.where(even_core, image_l, image_r))
    both = own.astype(f32) + came.astype(f32)
    tt_hi, tt_lo = two_parts(both[544] + both[545])
    uu_hi, uu_lo = two_parts(both[546] + both[547])
    sums = jnp.stack([tt_hi, tt_lo, uu_hi, uu_lo, both[548].astype(bf16)])
    pair = jnp.concatenate(
        [
            both[:512].astype(bf16).reshape(16, 32, 1024),
            jnp.broadcast_to(sums[None], (16, 5, 1024)),
            both[512:544].astype(bf16).reshape(16, 2, 1024),
            jnp.zeros((16, 1, 1024), bf16),
        ],
        axis=1,
    )
    total = jnp.sum(exchange(pair, CHIPS).astype(f32), axis=0)
    total, emb_t = lax.optimization_barrier((total, emb_t))
    sum_tt = total[32] + total[33]
    scale_t = 1.0 / (root * jnp.sqrt(sum_tt / D + 1e-06))
    inverse_u = 1.0 / (root * jnp.sqrt((total[34] + total[35]) / D + 1e-06))
    scale_u = inverse_u[:, None]
    uhat = u * scale_u
    uhat_b = uhat.astype(bf16)
    cosv = total[36] * scale_t * inverse_u
    gram_u = gram_raw * inverse_u[None, :] * lax.dynamic_slice_in_dim(inverse_u, first, 32)[:, None]
    scale_rows = lax.dynamic_slice_in_dim(scale_t, first, 32)
    diff = (gram_u - total[:32] * scale_t[None, :] * scale_rows[:, None]).astype(bf16)
    inner = 4.0 * jnp.sum(diff.astype(f32) * gram_u, axis=1) - lax.dynamic_slice_in_dim(
        cosv, first, 32
    )
    in_hi, in_lo = two_parts(inner)
    block = jnp.concatenate(
        [
            diff,
            total[37:39].astype(bf16),
            jnp.pad(jnp.concatenate([in_hi, in_lo])[None], ((0, 5), (0, 960))),
        ]
    )
    block = share(block, CHIPS, 16)
    even, odd = ordered(core, block, swap(block, "core"))
    diff_b = jnp.concatenate([even[:, :32].reshape(512, 1024), odd[:, :32].reshape(512, 1024)])
    near = lax.dynamic_slice_in_dim(even, xh * 8, 8)[:, 32:34].reshape(32, 512)
    far = lax.dynamic_slice_in_dim(odd, xh * 8, 8)[:, 32:34].reshape(32, 512)
    image_t = jnp.concatenate([near, far], axis=1)
    in_hi = jnp.concatenate([even[:, 34, :32], odd[:, 34, :32]]).reshape(1024)
    in_lo = jnp.concatenate([even[:, 34, 32:64], odd[:, 34, 32:64]]).reshape(1024)
    inner = in_hi.astype(f32) + in_lo.astype(f32)
    teach2 = jnp.concatenate(ordered(xh, teach, teach_other), axis=1)
    diff_f = diff_b.astype(f32)
    loss = 1.0 - jnp.sum(cosv) / 1024 + jnp.sum(diff_f * diff_f) / 1024

    grad_hat = 4.0 * jnp.dot(diff_b, uhat_b, preferred_element_type=f32) - (
        teach2.astype(f32) * scale_t[:, None]
    )
    du = (grad_hat - uhat * inner[:, None]) * scale_u
    du = (du * (grad_scale / 1024)).astype(bf16)
    grad_proj = jnp.dot(emb_t, du, preferred_element_type=f32)

    mask = chosen.astype(f32)
    scale_t_d = jnp.sum(mask * scale_t[None, :], axis=1, keepdims=True)
    scale_u_d = jnp.sum(mask * inverse_u[None, :], axis=1, keepdims=True)
    inner_d = jnp.sum(mask * inner[None, :], axis=1, keepdims=True)
    diff_d = jnp.dot(chosen, diff_b, preferred_element_type=f32) * inverse_u[None, :]
    mixed = jnp.dot(diff_d.astype(bf16), emb, preferred_element_type=f32).astype(bf16)
    student = (
        4.0 * jnp.dot(mixed, product, preferred_element_type=f32)
        - scale_t_d * image_t.astype(f32)
        - inner_d * scale_u_d * image_d
    )
    grad_student = student * scale_u_d * (grad_scale / 1024)
    return (grad_proj, grad_student, loss)


def solution(mesh):
    fine = Mesh(mesh.devices.reshape(4, 2, 16, 2, 2), ("y", "core", "z", "xh", "xl"))
    dp = ("z", "xh")
    placed = (
        P(dp, ROW),
        P(dp, ROW),
        P(ROW, dp),
        P(),
        P(dp, None),
        P(dp, None),
        P(dp, None),
        P(None, ROW),
    )
    return jax.shard_map(
        on_device,
        mesh=fine,
        in_specs=placed,
        out_specs=(P(None, ROW), P(dp, None), P()),
        check_vma=False,
    )
```

```python
import jax
import jax.numpy as jnp
from jax import lax
from jax.experimental import pallas as pl
from jax.experimental.pallas import tpu as pltpu
from jax.sharding import Mesh, PartitionSpec as P

D = 4096
grad_scale = 262144.0
f32, bf16 = jnp.float32, jnp.bfloat16

ROW = ("y", "core", "xl")
HALF = ("y", "xl")
PLANE = ("y", "core", "xh", "xl")
CHIPS = ("y", "xl", "xh")
NT = (((1,), (1,)), ((), ()))
TN = (((0,), (0,)), ((), ()))


def swap(value, axis):
    return lax.ppermute(value, axis, [(0, 1), (1, 0)])


def exchange(value, axes):
    return lax.all_to_all(value, axes, split_axis=0, concat_axis=0)


def share(value, axes, count):
    return exchange(jnp.broadcast_to(value[None], (count,) + value.shape), axes)


def two_parts(value):
    high = lax.reduce_precision(value, 8, 7)
    return high.astype(bf16), (value - high).astype(bf16)


def ordered(index, own, other):
    first = index == 0
    return jnp.where(first, own, other), jnp.where(first, other, own)


def part_kernel(core_ref, hidden_ref, weight_ref, out_ref):
    both = jnp.concatenate([weight_ref[0], weight_ref[1]], axis=1)
    got = jnp.dot(hidden_ref[...], both, preferred_element_type=f32).astype(bf16)
    out_ref[0] = got[:, :128]
    out_ref[1] = got[:, 128:]


def parts_for(core, hidden, weight):
    tokens, depth = hidden.shape
    assert weight.shape[1] >= depth
    return pl.pallas_call(
        part_kernel,
        grid_spec=pltpu.PrefetchScalarGridSpec(
            num_scalar_prefetch=1,
            grid=(4,),
            in_specs=[
                pl.BlockSpec((tokens, depth), lambda i, c: (0, 0)),
                pl.BlockSpec((2, depth, 128), lambda i, c: (2 * i + c[0], 0, 0)),
            ],
            out_specs=pl.BlockSpec((2, tokens, 128), lambda i, c: (i, 0, 0)),
        ),
        out_shape=jax.ShapeDtypeStruct((8, tokens, 128), bf16),
        compiler_params=pltpu.CompilerParams(vmem_limit_bytes=56 << 20),
        cost_estimate=pl.CostEstimate(
            flops=2 * tokens * depth * 1024, bytes_accessed=5_000_000, transcendentals=0
        ),
    )(core.reshape(1).astype(jnp.int32), hidden, weight)


def on_device(
    hidden, residual, down_weight, norm_gain, seq_lengths, owner_slot, student_emb, proj_weight
):
    core, xh, z = lax.axis_index("core"), lax.axis_index("xh"), lax.axis_index("z")
    rank = lax.axis_index(ROW)
    root = jnp.sqrt(f32(D))
    low = xh == 0

    slabs = student_emb.reshape(32, 8, 128).transpose(1, 0, 2).reshape(256, 128)
    weight = lax.all_gather(jnp.concatenate([down_weight, slabs]), "z", axis=0)

    left, right = residual[:, :128], residual[:, 128:]
    mine, theirs = jnp.where(low, left, right), jnp.where(low, right, left)
    table = jnp.pad(
        jnp.concatenate([seq_lengths, owner_slot], axis=1).astype(bf16), ((0, 15), (0, 64))
    )
    came = swap(jnp.concatenate([theirs, table], axis=0), "xh")
    residual2 = jnp.concatenate(ordered(xh, mine, came[:448]), axis=0)
    table2 = jnp.concatenate(ordered(xh, table[:1], came[448:449]), axis=0).astype(jnp.int32)
    lengths, owners = table2[:, :32], table2[:, 32:64]
    starts = jnp.cumsum(lengths, axis=1) - lengths
    places = jnp.arange(448, dtype=jnp.int32)
    inside = (places[None, None, :] >= starts[:, :, None]) & (
        places[None, None, :] < (starts + lengths)[:, :, None]
    )
    slot = jnp.arange(32, dtype=jnp.int32)
    slot = (slot % 16) * 2 + slot // 16
    select = (owners[:, None, :] == slot[None, :, None]).astype(bf16)
    member = jnp.einsum("bdi,bit->bdt", select, inside.astype(bf16), preferred_element_type=f32)
    empty = jnp.zeros((32, 448), f32)
    pool = jnp.stack(
        [
            jnp.concatenate([member[0], empty], axis=1),
            jnp.concatenate([empty, member[1]], axis=1),
        ],
        axis=1,
    ).reshape(64, 896)
    count = jnp.sum(pool, axis=1, keepdims=True)
    pool = pool.astype(bf16)

    def product_rows(which):
        return lax.dot_general(
            lax.dynamic_slice_in_dim(proj_weight, which * 512, 512, axis=0),
            proj_weight,
            NT,
            preferred_element_type=f32,
        ).astype(bf16)

    product = swap(product_rows(1 - core), "core").astype(f32)
    product = (product + product_rows(core).astype(f32)).astype(bf16)
    product, hidden, pool, count, residual2 = lax.optimization_barrier(
        (product, hidden, pool, count, residual2)
    )
    hidden2 = jnp.concatenate(ordered(xh, hidden, swap(hidden, "xh")), axis=0)
    product = jnp.sum(exchange(product.reshape(8, 64, 1024), HALF).astype(f32), axis=0)
    product = share(product.astype(bf16), HALF, 8).reshape(512, 1024)
    product = jnp.concatenate(ordered(core, product, swap(product, "core")))
    hidden2, product = lax.optimization_barrier((hidden2, product))

    proj_own = jnp.where(low, proj_weight[:, :128], proj_weight[:, 128:])
    gain = lax.dynamic_slice_in_dim(norm_gain, rank * 256 + xh * 128, 128)
    pick = jnp.arange(1024, dtype=jnp.int32)
    place = pick // 2 % 32
    chosen = (pick // 64 * 2 + pick % 2)[None, :] == jnp.arange(32, dtype=jnp.int32)[:, None]
    student_of = place[None, :]
    source = place * 32 + pick // 64 * 2 + pick % 2
    order = (source[:, None] == pick[None, :]).astype(bf16)
    chosen2 = jnp.concatenate([chosen & (student_of == z), chosen & (student_of == 16 + z)]).astype(bf16)
    chosen = (chosen & (student_of == xh * 16 + z)).astype(bf16)

    slabs = weight[:, 896:]
    far = swap(lax.dynamic_slice_in_dim(slabs, core * 8, 8), "xh")
    part_theirs = swap(parts_for(1 - core, hidden2, weight), "core")
    part_mine = parts_for(core, hidden2, weight)
    pair = (part_mine.astype(f32) + part_theirs.astype(f32)).astype(bf16)
    y = jnp.sum(exchange(pair, HALF).astype(f32), axis=0) + residual2.astype(f32)

    squares = jnp.sum(y * y, axis=1).reshape(7, 128)
    squares = jnp.sum(share(squares, PLANE, 32), axis=0).reshape(896)
    squares, far = lax.optimization_barrier((squares, far))
    far = jnp.concatenate(ordered(core, far, swap(far, "core")))
    emb = jnp.concatenate(ordered(xh, slabs, far)).reshape(32, 8, 32, 128)
    emb = emb.transpose(0, 2, 1, 3).reshape(1024, 1024)
    normed = (y * lax.rsqrt(squares / D + 1e-05)[:, None] * gain).astype(bf16)
    pooled = (jnp.dot(pool, normed, preferred_element_type=f32) / count).astype(bf16)
    teach = share(pooled, "z", 16).reshape(1024, 128)
    teach_other = swap(teach, "xh")

    emb = jnp.dot(order, emb, preferred_element_type=f32).astype(bf16)
    u = jnp.dot(emb, proj_weight, preferred_element_type=f32)
    u_own = jnp.where(low, u[:, :128], u[:, 128:])
    uu_hi, uu_lo = two_parts(jnp.sum(u_own * u_own, axis=1))
    first = core * 512 + lax.axis_index(CHIPS) * 32
    image = jnp.dot(emb, product, preferred_element_type=f32).astype(bf16)
    gram_raw = lax.dot_general(
        lax.dynamic_slice_in_dim(image, first, 32), emb, NT, preferred_element_type=f32
    )
    image_d = jnp.dot(student_emb, product, preferred_element_type=f32)

    def rows_of(which):
        return lax.dot_general(
            lax.dynamic_slice_in_dim(teach, which * 512, 512, axis=0),
            teach,
            NT,
            preferred_element_type=f32,
        ).astype(bf16)

    tch = teach.astype(f32)
    sum_tt = jnp.sum(tch * tch, axis=1)
    cross = jnp.sum(tch * u_own, axis=1).astype(bf16)
    tt_hi, tt_lo = two_parts(sum_tt)
    teach_d = jnp.dot(chosen2, teach, preferred_element_type=f32).astype(bf16)
    image_t = lax.dot_general(teach_d, proj_own, NT, preferred_element_type=f32).astype(bf16)
    image_l, image_r = image_t[:, :512].reshape(32, 1024), image_t[:, 512:].reshape(32, 1024)
    even_core = core == 0
    sums = jnp.stack([tt_hi, tt_lo, uu_hi, uu_lo, cross])

    def packet(which, image_half):
        return jnp.concatenate([rows_of(which), image_half, jnp.pad(sums, ((0, 3), (0, 0)))])

    came = swap(packet(1 - core, jnp.where(even_core, image_r, image_l)), "core")
    own = packet(core, jnp.where(even_core, image_l, image_r))
    both = own.astype(f32) + came.astype(f32)
    tt_hi, tt_lo = two_parts(both[544] + both[545])
    uu_hi, uu_lo = two_parts(both[546] + both[547])
    sums = jnp.stack([tt_hi, tt_lo, uu_hi, uu_lo, both[548].astype(bf16)])
    pair = jnp.concatenate(
        [
            both[:512].astype(bf16).reshape(16, 32, 1024),
            jnp.broadcast_to(sums[None], (16, 5, 1024)),
            both[512:544].astype(bf16).reshape(16, 2, 1024),
            jnp.zeros((16, 1, 1024), bf16),
        ],
        axis=1,
    )
    total = jnp.sum(exchange(pair, CHIPS).astype(f32), axis=0)
    sum_tt = total[32] + total[33]
    scale_t = 1.0 / (root * jnp.sqrt(sum_tt / D + 1e-06))
    inverse_u = 1.0 / (root * jnp.sqrt((total[34] + total[35]) / D + 1e-06))
    scale_u = inverse_u[:, None]
    uhat = u * scale_u
    uhat_b = uhat.astype(bf16)
    cosv = total[36] * scale_t * inverse_u
    gram_u = gram_raw * inverse_u[None, :] * lax.dynamic_slice_in_dim(inverse_u, first, 32)[:, None]
    scale_rows = lax.dynamic_slice_in_dim(scale_t, first, 32)
    diff = (gram_u - total[:32] * scale_t[None, :] * scale_rows[:, None]).astype(bf16)
    inner = 4.0 * jnp.sum(diff.astype(f32) * gram_u, axis=1) - lax.dynamic_slice_in_dim(
        cosv, first, 32
    )
    in_hi, in_lo = two_parts(inner)
    block = jnp.concatenate(
        [
            diff,
            total[37:39].astype(bf16),
            jnp.pad(jnp.concatenate([in_hi, in_lo])[None], ((0, 5), (0, 960))),
        ]
    )
    block, teach_other = lax.optimization_barrier((block, teach_other))
    block = share(block, CHIPS, 16)
    even, odd = ordered(core, block, swap(block, "core"))
    diff_b = jnp.concatenate([even[:, :32].reshape(512, 1024), odd[:, :32].reshape(512, 1024)])
    near = lax.dynamic_slice_in_dim(even, xh * 8, 8)[:, 32:34].reshape(32, 512)
    far = lax.dynamic_slice_in_dim(odd, xh * 8, 8)[:, 32:34].reshape(32, 512)
    image_t = jnp.concatenate([near, far], axis=1)
    in_hi = jnp.concatenate([even[:, 34, :32], odd[:, 34, :32]]).reshape(1024)
    in_lo = jnp.concatenate([even[:, 34, 32:64], odd[:, 34, 32:64]]).reshape(1024)
    inner = in_hi.astype(f32) + in_lo.astype(f32)
    teach2 = jnp.concatenate(ordered(xh, teach, teach_other), axis=1)
    diff_f = diff_b.astype(f32)
    loss = 1.0 - jnp.sum(cosv) / 1024 + jnp.sum(diff_f * diff_f) / 1024

    grad_hat = 4.0 * jnp.dot(diff_b, uhat_b, preferred_element_type=f32) - (
        teach2.astype(f32) * scale_t[:, None]
    )
    du = (grad_hat - uhat * inner[:, None]) * scale_u
    du = (du * (grad_scale / 1024)).astype(bf16)
    grad_proj = lax.dot_general(emb, du, TN, preferred_element_type=f32)

    mask = chosen.astype(f32)
    scale_t_d = jnp.sum(mask * scale_t[None, :], axis=1, keepdims=True)
    scale_u_d = jnp.sum(mask * inverse_u[None, :], axis=1, keepdims=True)
    inner_d = jnp.sum(mask * inner[None, :], axis=1, keepdims=True)
    diff_d = jnp.dot(chosen, diff_b, preferred_element_type=f32) * inverse_u[None, :]
    student = (
        4.0 * jnp.dot(diff_d.astype(bf16), image, preferred_element_type=f32)
        - scale_t_d * image_t.astype(f32)
        - inner_d * scale_u_d * image_d
    )
    grad_student = student * scale_u_d * (grad_scale / 1024)
    return (grad_proj, grad_student, loss)


def solution(mesh):
    fine = Mesh(mesh.devices.reshape(4, 2, 16, 2, 2), ("y", "core", "z", "xh", "xl"))
    dp = ("z", "xh")
    placed = (
        P(dp, ROW),
        P(dp, ROW),
        P(ROW, dp),
        P(),
        P(dp, None),
        P(dp, None),
        P(dp, None),
        P(None, ROW),
    )
    return jax.shard_map(
        on_device,
        mesh=fine,
        in_specs=placed,
        out_specs=(P(None, ROW), P(dp, None), P()),
        check_vma=False,
    )
```

```python
import jax
import jax.numpy as jnp
from jax import lax
from jax.experimental import pallas as pl
from jax.experimental.pallas import tpu as pltpu
from jax.sharding import Mesh, PartitionSpec as P

D = 4096
grad_scale = 262144.0
f32, bf16 = jnp.float32, jnp.bfloat16

ROW = ("y", "core", "xl")
HALF = ("y", "xl")
PLANE = ("y", "core", "xh", "xl")
CHIPS = ("y", "xl", "xh")
NT = (((1,), (1,)), ((), ()))
TN = (((0,), (0,)), ((), ()))


def swap(value, axis):
    return lax.ppermute(value, axis, [(0, 1), (1, 0)])


def exchange(value, axes):
    return lax.all_to_all(value, axes, split_axis=0, concat_axis=0)


def share(value, axes, count):
    return exchange(jnp.broadcast_to(value[None], (count,) + value.shape), axes)


def two_parts(value):
    high = lax.reduce_precision(value, 8, 7)
    return high.astype(bf16), (value - high).astype(bf16)


def slab_rows(slabs):
    return slabs.reshape(-1, 8, 32, 128).transpose(0, 2, 1, 3).reshape(-1, 1024)


def ordered(index, own, other):
    first = index == 0
    return jnp.where(first, own, other), jnp.where(first, other, own)


def part_kernel(core_ref, hidden_ref, weight_ref, out_ref):
    both = jnp.concatenate([weight_ref[0], weight_ref[1]], axis=1)
    got = jnp.dot(hidden_ref[...], both, preferred_element_type=f32).astype(bf16)
    out_ref[0] = got[:, :128]
    out_ref[1] = got[:, 128:]


def parts_for(core, hidden, weight):
    tokens, depth = hidden.shape
    assert weight.shape[1] >= depth
    return pl.pallas_call(
        part_kernel,
        grid_spec=pltpu.PrefetchScalarGridSpec(
            num_scalar_prefetch=1,
            grid=(4,),
            in_specs=[
                pl.BlockSpec((tokens, depth), lambda i, c: (0, 0)),
                pl.BlockSpec((2, depth, 128), lambda i, c: (2 * i + c[0], 0, 0)),
            ],
            out_specs=pl.BlockSpec((2, tokens, 128), lambda i, c: (i, 0, 0)),
        ),
        out_shape=jax.ShapeDtypeStruct((8, tokens, 128), bf16),
        compiler_params=pltpu.CompilerParams(vmem_limit_bytes=32 << 20),
        cost_estimate=pl.CostEstimate(
            flops=2 * tokens * depth * 1024, bytes_accessed=5_000_000, transcendentals=0
        ),
    )(core.reshape(1).astype(jnp.int32), hidden, weight)


def on_device(
    hidden, residual, down_weight, norm_gain, seq_lengths, owner_slot, student_emb, proj_weight
):
    core, xh, z = lax.axis_index("core"), lax.axis_index("xh"), lax.axis_index("z")
    rank = lax.axis_index(ROW)
    root = jnp.sqrt(f32(D))
    low = xh == 0

    slabs = student_emb.reshape(32, 8, 128).transpose(1, 0, 2).reshape(256, 128)
    weight = lax.all_gather(jnp.concatenate([down_weight, slabs]), "z", axis=0)

    left, right = residual[:, :128], residual[:, 128:]
    mine, theirs = jnp.where(low, left, right), jnp.where(low, right, left)
    table = jnp.pad(
        jnp.concatenate([seq_lengths, owner_slot], axis=1).astype(bf16), ((0, 15), (0, 64))
    )
    came = swap(jnp.concatenate([theirs, table], axis=0), "xh")
    residual2 = jnp.concatenate(ordered(xh, mine, came[:448]), axis=0)
    table2 = jnp.concatenate(ordered(xh, table[:1], came[448:449]), axis=0).astype(jnp.int32)
    lengths, owners = table2[:, :32], table2[:, 32:64]
    starts = jnp.cumsum(lengths, axis=1) - lengths
    places = jnp.arange(448, dtype=jnp.int32)
    inside = (places[None, None, :] >= starts[:, :, None]) & (
        places[None, None, :] < (starts + lengths)[:, :, None]
    )
    slot = jnp.arange(32, dtype=jnp.int32)
    slot = (slot % 16) * 2 + slot // 16
    select = (owners[:, None, :] == slot[None, :, None]).astype(bf16)
    member = jnp.einsum("bdi,bit->bdt", select, inside.astype(bf16), preferred_element_type=f32)
    empty = jnp.zeros((32, 448), f32)
    pool = jnp.stack(
        [
            jnp.concatenate([member[0], empty], axis=1),
            jnp.concatenate([empty, member[1]], axis=1),
        ],
        axis=1,
    ).reshape(64, 896)
    count = jnp.sum(pool, axis=1, keepdims=True)
    pool = pool.astype(bf16)

    def product_rows(which):
        return lax.dot_general(
            lax.dynamic_slice_in_dim(proj_weight, which * 512, 512, axis=0),
            proj_weight,
            NT,
            preferred_element_type=f32,
        ).astype(bf16)

    product = swap(product_rows(1 - core), "core").astype(f32)
    product = (product + product_rows(core).astype(f32)).astype(bf16)
    product, hidden, pool, count, residual2 = lax.optimization_barrier(
        (product, hidden, pool, count, residual2)
    )
    hidden2 = jnp.concatenate(ordered(xh, hidden, swap(hidden, "xh")), axis=0)
    product = jnp.sum(exchange(product.reshape(8, 64, 1024), HALF).astype(f32), axis=0)
    product = share(product.astype(bf16), HALF, 8).reshape(512, 1024)
    product = jnp.concatenate(ordered(core, product, swap(product, "core")))
    hidden2, product = lax.optimization_barrier((hidden2, product))

    proj_own = jnp.where(low, proj_weight[:, :128], proj_weight[:, 128:])
    gain = lax.dynamic_slice_in_dim(norm_gain, rank * 256 + xh * 128, 128)
    pick = jnp.arange(1024, dtype=jnp.int32)
    place = pick // 2 % 32
    chosen = (pick // 64 * 2 + pick % 2)[None, :] == jnp.arange(32, dtype=jnp.int32)[:, None]
    student_of = place[None, :]
    block = jnp.where(
        place // 16 == xh,
        place % 16,
        place % 8 + jnp.where(place % 16 // 8 == core, 16, 24),
    )
    source = block * 32 + pick // 64 * 2 + pick % 2
    order = (source[:, None] == pick[None, :]).astype(bf16)
    chosen2 = jnp.concatenate([chosen & (student_of == z), chosen & (student_of == 16 + z)]).astype(bf16)
    chosen = (chosen & (student_of == xh * 16 + z)).astype(bf16)

    slabs = weight[:, 896:]
    far = swap(lax.dynamic_slice_in_dim(slabs, core * 8, 8), "xh")
    part_theirs = swap(parts_for(1 - core, hidden2, weight), "core")
    part_mine = parts_for(core, hidden2, weight)
    pair = (part_mine.astype(f32) + part_theirs.astype(f32)).astype(bf16)
    y = jnp.sum(exchange(pair, HALF).astype(f32), axis=0) + residual2.astype(f32)

    y, near = lax.optimization_barrier((y, slab_rows(slabs)))
    squares = jnp.sum(y * y, axis=1).reshape(7, 128)
    squares = jnp.sum(share(squares, PLANE, 32), axis=0).reshape(896)
    squares, far = lax.optimization_barrier((squares, far))
    emb = jnp.concatenate([near, slab_rows(far), slab_rows(swap(far, "core"))])
    normed = (y * lax.rsqrt(squares / D + 1e-05)[:, None] * gain).astype(bf16)
    pooled = (jnp.dot(pool, normed, preferred_element_type=f32) / count).astype(bf16)
    teach = share(pooled, "z", 16).reshape(1024, 128)
    teach_other = swap(teach, "xh")

    emb = jnp.dot(order, emb, preferred_element_type=f32).astype(bf16)
    u = jnp.dot(emb, proj_weight, preferred_element_type=f32)
    u_own = jnp.where(low, u[:, :128], u[:, 128:])
    uu_hi, uu_lo = two_parts(jnp.sum(u_own * u_own, axis=1))
    first = core * 512 + lax.axis_index(CHIPS) * 32
    image = jnp.dot(emb, product, preferred_element_type=f32).astype(bf16)
    gram_raw = lax.dot_general(
        lax.dynamic_slice_in_dim(image, first, 32), emb, NT, preferred_element_type=f32
    )
    image_d = jnp.dot(student_emb, product, preferred_element_type=f32)

    def rows_of(which):
        return lax.dot_general(
            lax.dynamic_slice_in_dim(teach, which * 512, 512, axis=0),
            teach,
            NT,
            preferred_element_type=f32,
        ).astype(bf16)

    tch = teach.astype(f32)
    sum_tt = jnp.sum(tch * tch, axis=1)
    cross = jnp.sum(tch * u_own, axis=1).astype(bf16)
    tt_hi, tt_lo = two_parts(sum_tt)
    teach_d = jnp.dot(chosen2, teach, preferred_element_type=f32).astype(bf16)
    image_t = lax.dot_general(teach_d, proj_own, NT, preferred_element_type=f32).astype(bf16)
    image_l, image_r = image_t[:, :512].reshape(32, 1024), image_t[:, 512:].reshape(32, 1024)
    even_core = core == 0
    sums = jnp.stack([tt_hi, tt_lo, uu_hi, uu_lo, cross])

    def packet(which, image_half):
        return jnp.concatenate([rows_of(which), image_half, jnp.pad(sums, ((0, 3), (0, 0)))])

    came = swap(packet(1 - core, jnp.where(even_core, image_r, image_l)), "core")
    own = packet(core, jnp.where(even_core, image_l, image_r))
    both = own.astype(f32) + came.astype(f32)
    tt_hi, tt_lo = two_parts(both[544] + both[545])
    uu_hi, uu_lo = two_parts(both[546] + both[547])
    sums = jnp.stack([tt_hi, tt_lo, uu_hi, uu_lo, both[548].astype(bf16)])
    pair = jnp.concatenate(
        [
            both[:512].astype(bf16).reshape(16, 32, 1024),
            jnp.broadcast_to(sums[None], (16, 5, 1024)),
            both[512:544].astype(bf16).reshape(16, 2, 1024),
            jnp.zeros((16, 1, 1024), bf16),
        ],
        axis=1,
    )
    total = jnp.sum(exchange(pair, CHIPS).astype(f32), axis=0)
    sum_tt = total[32] + total[33]
    scale_t = 1.0 / (root * jnp.sqrt(sum_tt / D + 1e-06))
    inverse_u = 1.0 / (root * jnp.sqrt((total[34] + total[35]) / D + 1e-06))
    scale_u = inverse_u[:, None]
    uhat = u * scale_u
    uhat_b = uhat.astype(bf16)
    cosv = total[36] * scale_t * inverse_u
    gram_u = gram_raw * inverse_u[None, :] * lax.dynamic_slice_in_dim(inverse_u, first, 32)[:, None]
    scale_rows = lax.dynamic_slice_in_dim(scale_t, first, 32)
    diff = (gram_u - total[:32] * scale_t[None, :] * scale_rows[:, None]).astype(bf16)
    inner = 4.0 * jnp.sum(diff.astype(f32) * gram_u, axis=1) - lax.dynamic_slice_in_dim(
        cosv, first, 32
    )
    in_hi, in_lo = two_parts(inner)
    block = jnp.concatenate(
        [
            diff,
            total[37:39].astype(bf16),
            jnp.pad(jnp.concatenate([in_hi, in_lo])[None], ((0, 5), (0, 960))),
        ]
    )
    block, teach_other = lax.optimization_barrier((block, teach_other))
    block = share(block, CHIPS, 16)
    even, odd = ordered(core, block, swap(block, "core"))
    diff_b = jnp.concatenate([even[:, :32].reshape(512, 1024), odd[:, :32].reshape(512, 1024)])
    near = lax.dynamic_slice_in_dim(even, xh * 8, 8)[:, 32:34].reshape(32, 512)
    far = lax.dynamic_slice_in_dim(odd, xh * 8, 8)[:, 32:34].reshape(32, 512)
    image_t = jnp.concatenate([near, far], axis=1)
    in_hi = jnp.concatenate([even[:, 34, :32], odd[:, 34, :32]]).reshape(1024)
    in_lo = jnp.concatenate([even[:, 34, 32:64], odd[:, 34, 32:64]]).reshape(1024)
    inner = in_hi.astype(f32) + in_lo.astype(f32)
    teach2 = jnp.concatenate(ordered(xh, teach, teach_other), axis=1)
    diff_f = diff_b.astype(f32)
    loss = 1.0 - jnp.sum(cosv) / 1024 + jnp.sum(diff_f * diff_f) / 1024

    grad_hat = 4.0 * jnp.dot(diff_b, uhat_b, preferred_element_type=f32) - (
        teach2.astype(f32) * scale_t[:, None]
    )
    du = (grad_hat - uhat * inner[:, None]) * scale_u
    du = (du * (grad_scale / 1024)).astype(bf16)
    grad_proj = lax.dot_general(emb, du, TN, preferred_element_type=f32)

    mask = chosen.astype(f32)
    scale_t_d = jnp.sum(mask * scale_t[None, :], axis=1, keepdims=True)
    scale_u_d = jnp.sum(mask * inverse_u[None, :], axis=1, keepdims=True)
    inner_d = jnp.sum(mask * inner[None, :], axis=1, keepdims=True)
    diff_d = jnp.dot(chosen, diff_b, preferred_element_type=f32) * inverse_u[None, :]
    student = (
        4.0 * jnp.dot(diff_d.astype(bf16), image, preferred_element_type=f32)
        - scale_t_d * image_t.astype(f32)
        - inner_d * scale_u_d * image_d
    )
    grad_student = student * scale_u_d * (grad_scale / 1024)
    return (grad_proj, grad_student, loss)


def solution(mesh):
    fine = Mesh(mesh.devices.reshape(4, 2, 16, 2, 2), ("y", "core", "z", "xh", "xl"))
    dp = ("z", "xh")
    placed = (
        P(dp, ROW),
        P(dp, ROW),
        P(ROW, dp),
        P(),
        P(dp, None),
        P(dp, None),
        P(dp, None),
        P(None, ROW),
    )
    return jax.shard_map(
        on_device,
        mesh=fine,
        in_specs=placed,
        out_specs=(P(None, ROW), P(dp, None), P()),
        check_vma=False,
    )
```

```python
import jax
import jax.numpy as jnp
from jax import lax
from jax.experimental import pallas as pl
from jax.experimental.pallas import tpu as pltpu
from jax.sharding import Mesh, PartitionSpec as P

D = 4096
grad_scale = 262144.0
f32, bf16 = jnp.float32, jnp.bfloat16

ROW = ("y", "core", "xl")
HALF = ("y", "xl")
PLANE = ("y", "core", "xh", "xl")
CHIPS = ("y", "xl", "xh")
NT = (((1,), (1,)), ((), ()))
TN = (((0,), (0,)), ((), ()))


def swap(value, axis):
    return lax.ppermute(value, axis, [(0, 1), (1, 0)])


def exchange(value, axes):
    return lax.all_to_all(value, axes, split_axis=0, concat_axis=0)


def share(value, axes, count):
    return exchange(jnp.broadcast_to(value[None], (count,) + value.shape), axes)


def two_parts(value):
    high = lax.reduce_precision(value, 8, 7)
    return high.astype(bf16), (value - high).astype(bf16)


def slab_rows(slabs):
    return slabs.reshape(-1, 8, 32, 128).transpose(0, 2, 1, 3).reshape(-1, 1024)


def ordered(index, own, other):
    first = index == 0
    return jnp.where(first, own, other), jnp.where(first, other, own)


def part_kernel(core_ref, hidden_ref, weight_ref, out_ref):
    both = jnp.concatenate([weight_ref[0], weight_ref[1]], axis=1)
    got = jnp.dot(hidden_ref[...], both, preferred_element_type=f32).astype(bf16)
    out_ref[0] = got[:, :128]
    out_ref[1] = got[:, 128:]


def parts_for(core, hidden, weight):
    tokens, depth = hidden.shape
    assert weight.shape[1] >= depth
    return pl.pallas_call(
        part_kernel,
        grid_spec=pltpu.PrefetchScalarGridSpec(
            num_scalar_prefetch=1,
            grid=(4,),
            in_specs=[
                pl.BlockSpec((tokens, depth), lambda i, c: (0, 0)),
                pl.BlockSpec((2, depth, 128), lambda i, c: (2 * i + c[0], 0, 0)),
            ],
            out_specs=pl.BlockSpec((2, tokens, 128), lambda i, c: (i, 0, 0)),
        ),
        out_shape=jax.ShapeDtypeStruct((8, tokens, 128), bf16),
        compiler_params=pltpu.CompilerParams(vmem_limit_bytes=32 << 20),
        cost_estimate=pl.CostEstimate(
            flops=2 * tokens * depth * 1024, bytes_accessed=5_000_000, transcendentals=0
        ),
    )(core.reshape(1).astype(jnp.int32), hidden, weight)


def on_device(
    hidden, residual, down_weight, norm_gain, seq_lengths, owner_slot, student_emb, proj_weight
):
    core, xh, z = lax.axis_index("core"), lax.axis_index("xh"), lax.axis_index("z")
    rank = lax.axis_index(ROW)
    root = jnp.sqrt(f32(D))
    low = xh == 0

    slabs = student_emb.reshape(32, 8, 128).transpose(1, 0, 2).reshape(256, 128)
    weight = lax.all_gather(jnp.concatenate([down_weight, slabs]), "z", axis=0)

    left, right = residual[:, :128], residual[:, 128:]
    mine, theirs = jnp.where(low, left, right), jnp.where(low, right, left)
    table = jnp.pad(
        jnp.concatenate([seq_lengths, owner_slot], axis=1).astype(bf16), ((0, 15), (0, 64))
    )
    came = swap(jnp.concatenate([theirs, table], axis=0), "xh")
    residual2 = jnp.concatenate(ordered(xh, mine, came[:448]), axis=0)
    table2 = jnp.concatenate(ordered(xh, table[:1], came[448:449]), axis=0).astype(jnp.int32)
    lengths, owners = table2[:, :32], table2[:, 32:64]
    starts = jnp.cumsum(lengths, axis=1) - lengths
    places = jnp.arange(448, dtype=jnp.int32)
    inside = (places[None, None, :] >= starts[:, :, None]) & (
        places[None, None, :] < (starts + lengths)[:, :, None]
    )
    slot = jnp.arange(32, dtype=jnp.int32)
    slot = (slot % 16) * 2 + slot // 16
    select = (owners[:, None, :] == slot[None, :, None]).astype(bf16)
    member = jnp.einsum("bdi,bit->bdt", select, inside.astype(bf16), preferred_element_type=f32)
    empty = jnp.zeros((32, 448), f32)
    pool = jnp.stack(
        [
            jnp.concatenate([member[0], empty], axis=1),
            jnp.concatenate([empty, member[1]], axis=1),
        ],
        axis=1,
    ).reshape(64, 896)
    count = jnp.sum(pool, axis=1, keepdims=True)
    pool = pool.astype(bf16)

    def product_rows(which):
        return lax.dot_general(
            lax.dynamic_slice_in_dim(proj_weight, which * 512, 512, axis=0),
            proj_weight,
            NT,
            preferred_element_type=f32,
        ).astype(bf16)

    product = swap(product_rows(1 - core), "core").astype(f32)
    product = (product + product_rows(core).astype(f32)).astype(bf16)
    product, hidden, pool, count, residual2 = lax.optimization_barrier(
        (product, hidden, pool, count, residual2)
    )
    hidden2 = jnp.concatenate(ordered(xh, hidden, swap(hidden, "xh")), axis=0)
    product = jnp.sum(exchange(product.reshape(8, 64, 1024), HALF).astype(f32), axis=0)
    product = share(product.astype(bf16), HALF, 8).reshape(512, 1024)
    product = jnp.concatenate(ordered(core, product, swap(product, "core")))
    hidden2, product = lax.optimization_barrier((hidden2, product))

    proj_own = jnp.where(low, proj_weight[:, :128], proj_weight[:, 128:])
    gain = lax.dynamic_slice_in_dim(norm_gain, rank * 256 + xh * 128, 128)
    pick = jnp.arange(1024, dtype=jnp.int32)
    place = pick // 2 % 32
    chosen = (pick // 64 * 2 + pick % 2)[None, :] == jnp.arange(32, dtype=jnp.int32)[:, None]
    student_of = place[None, :]
    block = jnp.where(
        place // 16 == xh,
        place % 16,
        place % 8 + jnp.where(place % 16 // 8 == core, 16, 24),
    )
    source = block * 32 + pick // 64 * 2 + pick % 2
    order = (source[:, None] == pick[None, :]).astype(bf16)
    chosen2 = jnp.concatenate([chosen & (student_of == z), chosen & (student_of == 16 + z)]).astype(bf16)
    chosen = (chosen & (student_of == xh * 16 + z)).astype(bf16)

    part_theirs = swap(parts_for(1 - core, hidden2, weight), "core")
    part_mine = parts_for(core, hidden2, weight)
    pair = (part_mine.astype(f32) + part_theirs.astype(f32)).astype(bf16)
    y = jnp.sum(exchange(pair, HALF).astype(f32), axis=0) + residual2.astype(f32)

    squares = jnp.sum(y * y, axis=1).reshape(7, 128)
    squares = jnp.sum(share(squares, PLANE, 32), axis=0).reshape(896)
    squares, slabs = lax.optimization_barrier((squares, weight[:, 896:]))
    far = swap(lax.dynamic_slice_in_dim(slabs, core * 8, 8), "xh")
    emb = jnp.concatenate([slab_rows(slabs), slab_rows(far), slab_rows(swap(far, "core"))])
    normed = (y * lax.rsqrt(squares / D + 1e-05)[:, None] * gain).astype(bf16)
    pooled = (jnp.dot(pool, normed, preferred_element_type=f32) / count).astype(bf16)
    teach = share(pooled, "z", 16).reshape(1024, 128)
    teach_other = swap(teach, "xh")

    emb = jnp.dot(order, emb, preferred_element_type=f32).astype(bf16)
    u = jnp.dot(emb, proj_weight, preferred_element_type=f32)
    u_own = jnp.where(low, u[:, :128], u[:, 128:])
    uu_hi, uu_lo = two_parts(jnp.sum(u_own * u_own, axis=1))
    first = core * 512 + lax.axis_index(CHIPS) * 32
    gram_raw = lax.dot_general(
        jnp.dot(
            lax.dynamic_slice_in_dim(emb, first, 32), product, preferred_element_type=f32
        ).astype(bf16),
        emb,
        NT,
        preferred_element_type=f32,
    )
    image_d = jnp.dot(student_emb, product, preferred_element_type=f32)

    def rows_of(which):
        return lax.dot_general(
            lax.dynamic_slice_in_dim(teach, which * 512, 512, axis=0),
            teach,
            NT,
            preferred_element_type=f32,
        ).astype(bf16)

    tch = teach.astype(f32)
    sum_tt = jnp.sum(tch * tch, axis=1)
    cross = jnp.sum(tch * u_own, axis=1).astype(bf16)
    tt_hi, tt_lo = two_parts(sum_tt)
    teach_d = jnp.dot(chosen2, teach, preferred_element_type=f32).astype(bf16)
    image_t = lax.dot_general(teach_d, proj_own, NT, preferred_element_type=f32).astype(bf16)
    image_l, image_r = image_t[:, :512].reshape(32, 1024), image_t[:, 512:].reshape(32, 1024)
    even_core = core == 0
    sums = jnp.stack([tt_hi, tt_lo, uu_hi, uu_lo, cross])

    def packet(which, image_half):
        return jnp.concatenate([rows_of(which), image_half, jnp.pad(sums, ((0, 3), (0, 0)))])

    came = swap(packet(1 - core, jnp.where(even_core, image_r, image_l)), "core")
    own = packet(core, jnp.where(even_core, image_l, image_r))
    both = own.astype(f32) + came.astype(f32)
    tt_hi, tt_lo = two_parts(both[544] + both[545])
    uu_hi, uu_lo = two_parts(both[546] + both[547])
    sums = jnp.stack([tt_hi, tt_lo, uu_hi, uu_lo, both[548].astype(bf16)])
    pair = jnp.concatenate(
        [
            both[:512].astype(bf16).reshape(16, 32, 1024),
            jnp.broadcast_to(sums[None], (16, 5, 1024)),
            both[512:544].astype(bf16).reshape(16, 2, 1024),
            jnp.zeros((16, 1, 1024), bf16),
        ],
        axis=1,
    )
    total = jnp.sum(exchange(pair, CHIPS).astype(f32), axis=0)
    sum_tt = total[32] + total[33]
    scale_t = 1.0 / (root * jnp.sqrt(sum_tt / D + 1e-06))
    inverse_u = 1.0 / (root * jnp.sqrt((total[34] + total[35]) / D + 1e-06))
    scale_u = inverse_u[:, None]
    uhat = u * scale_u
    uhat_b = uhat.astype(bf16)
    cosv = total[36] * scale_t * inverse_u
    gram_u = gram_raw * inverse_u[None, :] * lax.dynamic_slice_in_dim(inverse_u, first, 32)[:, None]
    scale_rows = lax.dynamic_slice_in_dim(scale_t, first, 32)
    diff = (gram_u - total[:32] * scale_t[None, :] * scale_rows[:, None]).astype(bf16)
    inner = 4.0 * jnp.sum(diff.astype(f32) * gram_u, axis=1) - lax.dynamic_slice_in_dim(
        cosv, first, 32
    )
    in_hi, in_lo = two_parts(inner)
    block = jnp.concatenate(
        [
            diff,
            total[37:39].astype(bf16),
            jnp.pad(jnp.concatenate([in_hi, in_lo])[None], ((0, 5), (0, 960))),
        ]
    )
    block, teach_other = lax.optimization_barrier((block, teach_other))
    block = share(block, CHIPS, 16)
    even, odd = ordered(core, block, swap(block, "core"))
    diff_b = jnp.concatenate([even[:, :32].reshape(512, 1024), odd[:, :32].reshape(512, 1024)])
    near = lax.dynamic_slice_in_dim(even, xh * 8, 8)[:, 32:34].reshape(32, 512)
    far = lax.dynamic_slice_in_dim(odd, xh * 8, 8)[:, 32:34].reshape(32, 512)
    image_t = jnp.concatenate([near, far], axis=1)
    in_hi = jnp.concatenate([even[:, 34, :32], odd[:, 34, :32]]).reshape(1024)
    in_lo = jnp.concatenate([even[:, 34, 32:64], odd[:, 34, 32:64]]).reshape(1024)
    inner = in_hi.astype(f32) + in_lo.astype(f32)
    teach2 = jnp.concatenate(ordered(xh, teach, teach_other), axis=1)
    diff_f = diff_b.astype(f32)
    loss = 1.0 - jnp.sum(cosv) / 1024 + jnp.sum(diff_f * diff_f) / 1024

    grad_hat = 4.0 * jnp.dot(diff_b, uhat_b, preferred_element_type=f32) - (
        teach2.astype(f32) * scale_t[:, None]
    )
    du = (grad_hat - uhat * inner[:, None]) * scale_u
    du = (du * (grad_scale / 1024)).astype(bf16)
    grad_proj = lax.dot_general(emb, du, TN, preferred_element_type=f32)

    mask = chosen.astype(f32)
    scale_t_d = jnp.sum(mask * scale_t[None, :], axis=1, keepdims=True)
    scale_u_d = jnp.sum(mask * inverse_u[None, :], axis=1, keepdims=True)
    inner_d = jnp.sum(mask * inner[None, :], axis=1, keepdims=True)
    diff_d = jnp.dot(chosen, diff_b, preferred_element_type=f32) * inverse_u[None, :]
    mixed = jnp.dot(diff_d.astype(bf16), emb, preferred_element_type=f32).astype(bf16)
    student = (
        4.0 * jnp.dot(mixed, product, preferred_element_type=f32)
        - scale_t_d * image_t.astype(f32)
        - inner_d * scale_u_d * image_d
    )
    grad_student = student * scale_u_d * (grad_scale / 1024)
    return (grad_proj, grad_student, loss)


def solution(mesh):
    fine = Mesh(mesh.devices.reshape(4, 2, 16, 2, 2), ("y", "core", "z", "xh", "xl"))
    dp = ("z", "xh")
    placed = (
        P(dp, ROW),
        P(dp, ROW),
        P(ROW, dp),
        P(),
        P(dp, None),
        P(dp, None),
        P(dp, None),
        P(None, ROW),
    )
    return jax.shard_map(
        on_device,
        mesh=fine,
        in_specs=placed,
        out_specs=(P(None, ROW), P(dp, None), P()),
        check_vma=False,
    )
```
